32 devices in a mesh: groups: 2 (over x), tp: 16 (over z, y, core).
Axes of the slice: x: 2, y: 2, z: 4, core: 2. Of those that a mesh axis runs over, the one named last changes fastest.
Arguments:
- residual: float32 [128, 16384], P(('groups', 'tp')), parts along dimension 0, may hold values from -36 to 36
- norm_gain: float32 [16384], replicated, may hold values from 0.1 to 1.9
- segment_ids: int32 [128], P('groups'), parts along dimension 0, may hold values from 0 to 3, never falling along the last dimension, each value on 1 to 32 neighbouring positions
- w_query: bfloat16 [16384, 8192], P(None, 'tp'), may hold values from -1.734375 to 1.734375
- w_key: bfloat16 [16384, 1024], P(None, 'tp'), may hold values from -0.046875 to 0.046875
- w_value: bfloat16 [16384, 1024], P(None, 'tp'), may hold values from -0.046875 to 0.046875
- w_out: bfloat16 [8192, 16384], P('tp'), may hold values from -0.1875 to 0.1875
Outputs:
- updated: float32 [128, 16384], P(('groups', 'tp')), parts along dimension 0
The draws below stay inside these ranges and needn't reach their ends.
There are 2 independent parts, one for each index of `groups`. The reference program is written for one: setup_inputs(seed, part) draws one part's arguments, and reference() takes and returns one part's arrays. A program takes and returns all parts, laid end to end along the dimension named above; an argument that names none is the same for every part. Nothing has to cross between parts.
All inputs are finite; a program needn't handle non-finite values.
Results may differ from the reference program's by a relative error of at most 0.014.
Values may be sent and summed in bfloat16 or wider, within the bound.
A program may use at most 128 MiB of HBM per device.

```python
import math
import jax
import jax.numpy as jnp
import numpy as np
from jax import lax

D = 16384
QH = 64
KVH = 8
HD = 128
BLOCK = 128
TOKENS = 64
N_TP = 16


def draw_w_key(key, part):
    key = jax.random.fold_in(key, 1)
    private = jnp.clip(jax.random.normal(key, (D, KVH * HD), jnp.float32), -6.0, 6.0) / math.sqrt(D)
    chosen = private
    chosen = chosen.reshape(D, KVH, HD).transpose(0, 2, 1).reshape(D, KVH * HD)
    return chosen.astype(jnp.bfloat16)


def draw_w_query(key, part):
    key = jax.random.fold_in(key, 2)
    key_noise = jax.random.fold_in(key, 0)
    private = jnp.clip(jax.random.normal(key_noise, (D, QH * HD), jnp.float32), -6.0, 6.0) / math.sqrt(D)
    return private.astype(jnp.bfloat16)


def draw_residual(key, part):
    key = jax.random.fold_in(key, 3)
    key_base, key_rows, key_cols = jax.random.split(key, 3)
    base_draw = jnp.clip(jax.random.normal(key_base, (TOKENS, D), jnp.float32), -6.0, 6.0)
    row_scale = jnp.exp(jax.random.uniform(key_rows, (TOKENS, 1), jnp.float32, math.log(0.3), math.log(3.0)))
    col_scale = jnp.exp(jax.random.uniform(key_cols, (1, D), jnp.float32, math.log(0.5), math.log(2.0)))
    return base_draw * row_scale * col_scale


def shard_levels(stream_key, extent, pieces, least, top_value):
    loudness, own = 1.0, jax.random.fold_in(stream_key, 6)
    for axis_at, shards_of in pieces:
        heights = jnp.exp(jax.random.uniform(jax.random.fold_in(own, axis_at), (shards_of,), jnp.float32, least / len(pieces), top_value / len(pieces)))
        loudness = loudness * jnp.repeat(heights, extent[axis_at] // shards_of).reshape([-1 if axis == axis_at else 1 for axis in range(len(extent))])
    return loudness


def split_up(count, total, bound, slope):
    weights = [(1 << 20) // math.isqrt(standing ** slope) + 1 for standing in range(2, count + 1)]
    rest, holding = total - bound - (count - 1), [1] * (count - 1)
    while rest > 0:
        free = [i for i in range(count - 1) if holding[i] < bound]
        pool, remaining = sum([weights[i] for i in free]), rest
        for i in free:
            more = min(bound - holding[i], max(1, remaining * weights[i] // pool), rest)
            holding[i] = holding[i] + more
            rest = rest - more
    return np.array([bound] + holding)


def uneven_parts(rng, amount, total, bound, skew):
    if amount == 2:
        one = jax.random.randint(rng, (), max(1, total - bound), min(bound, total - 1) + 1)
        return jnp.stack([one, total - one])
    sizes = jnp.asarray(split_up(amount, total, bound, skew), jnp.int32)
    couples = (amount - 1) // 2
    giver, taker = sizes[1:1 + 2 * couples:2], sizes[2:2 + 2 * couples:2]
    margin = jnp.minimum(giver - 1, bound - taker)
    shifted = jax.random.randint(jax.random.fold_in(rng, 1), (couples,), 0, 1 << 20) % (margin + 1)
    sizes = sizes.at[1:1 + 2 * couples:2].set(giver - shifted).at[2:2 + 2 * couples:2].set(taker + shifted)
    return sizes[jax.random.permutation(jax.random.fold_in(rng, 2), amount)]


def noise(key, extent, deviation, most, pieces=(), kind=jnp.bfloat16):
    entries = jax.random.normal(key, extent, jnp.float32) * deviation
    if len(pieces) > 0:
        entries = shard_levels(key, extent, pieces, -0.22, 0.18) * entries
    return jnp.clip(entries, min=-most, max=most).astype(kind)


def setup_inputs(seed: int = 0, part: int = 0) -> dict:
    streams_of = jax.random.split(jax.random.key(seed), 8)
    part_keys = jax.random.split(jax.random.fold_in(streams_of[7], part), 8)
    return {
        "residual": draw_residual(jax.random.fold_in(jax.random.fold_in(streams_of[7], part), 71), part),
        "norm_gain": jnp.clip(1.0 + 0.18 * jax.random.normal(streams_of[1], (D,), jnp.float32), 0.1, 1.9),
        "segment_ids": jnp.searchsorted(jnp.cumsum(uneven_parts(part_keys[2], 4, TOKENS, TOKENS // 2, 0)), jnp.arange(TOKENS), side="right").astype(jnp.int32),
        "w_query": draw_w_query(jax.random.fold_in(streams_of[7], 71), part),
        "w_key": draw_w_key(jax.random.fold_in(streams_of[7], 71), part),
        "w_value": noise(streams_of[5], (D, KVH * HD), D ** -0.5, 0.046875, ((1, 16),)),
        "w_out": noise(streams_of[6], (QH * HD, D), (QH * HD // 8) ** -0.5, 0.1875, ((0, 16),)),
    }


code_limit = 448.0
rope_base = 500000.0

def quantize(values):
    row_count = values.shape[0]
    blocks = values.reshape(row_count, -1, BLOCK)
    scales = ((lax.optimization_barrier(jnp.max(jnp.abs(blocks), axis=2)) + 1e-06) / code_limit).astype(jnp.bfloat16)
    encoded = (blocks / scales.astype(jnp.float32)[:, :, None]).astype(jnp.bfloat16)
    return (encoded.reshape(row_count, -1), scales)

def expand(encoded, scales):
    row_count = encoded.shape[0]
    blocks = encoded.astype(jnp.float32).reshape(row_count, -1, BLOCK) * scales.astype(jnp.float32)[:, :, None]
    return blocks.reshape(row_count, -1)

def positions_of(segment_ids):
    token_count = segment_ids.shape[0]
    token_index = jnp.arange(token_count, dtype=jnp.int32)
    change = jnp.concatenate([jnp.ones((1,), dtype=bool), segment_ids[1:] != segment_ids[:-1]])
    offset = lax.cummax(jnp.where(change, token_index, jnp.zeros_like(token_index)), axis=0)
    return (token_index - offset).astype(jnp.int32)

def rotate(values, positions):
    half_dim = values.shape[-1] // 2
    inv_freq = rope_base ** (-(jnp.arange(half_dim, dtype=jnp.float32) * 2.0) / (2 * half_dim))
    angles = positions.astype(jnp.float32)[:, None] * inv_freq[None, :]
    cosine = jnp.cos(angles)[:, None, :]
    sine_vals = jnp.sin(angles)[:, None, :]
    first_half = values[..., :half_dim].astype(jnp.float32)
    second = values[..., half_dim:].astype(jnp.float32)
    return jnp.concatenate([first_half * cosine - second * sine_vals, second * cosine + first_half * sine_vals], axis=-1)

def attend(queries, chosen_keys, chosen_values, segment_ids):
    token_count = queries.shape[0]
    token_index = jnp.arange(token_count, dtype=jnp.int32)
    scores = jnp.einsum('qhd,khd->hqk', queries.astype(jnp.float32), chosen_keys.astype(jnp.float32)) / math.sqrt(queries.shape[2])
    allowed = (token_index[None, :] <= token_index[:, None]) & (segment_ids[:, None] == segment_ids[None, :])
    scores = jnp.where(allowed[None], scores, -1e+30)
    row_max = lax.optimization_barrier(jnp.max(scores, axis=2, keepdims=True))
    weights = jnp.exp(scores - row_max)
    probabilities = (weights / lax.optimization_barrier(jnp.sum(weights, axis=2, keepdims=True))).astype(jnp.bfloat16)
    outputs = jnp.einsum('hqk,khd->qhd', probabilities.astype(jnp.float32), chosen_values.astype(jnp.float32))
    return outputs.astype(jnp.bfloat16).reshape(token_count, -1)

def reference(residual, norm_gain, segment_ids, w_query, w_key, w_value, w_out):
    mean_square = lax.optimization_barrier(jnp.mean(residual * residual, axis=1, keepdims=True))
    normed = residual * lax.rsqrt(mean_square + 1e-05) * norm_gain[None, :]
    encoded, scales = quantize(normed)
    inputs = expand(encoded, scales).astype(jnp.bfloat16)
    query_lin = jnp.dot(inputs, w_query, preferred_element_type=jnp.float32).astype(jnp.bfloat16)
    key_lin = jnp.dot(inputs, w_key, preferred_element_type=jnp.float32).astype(jnp.bfloat16)
    value_lin = jnp.dot(inputs, w_value, preferred_element_type=jnp.float32).astype(jnp.bfloat16)
    positions = positions_of(segment_ids)
    queries = rotate(query_lin.reshape(TOKENS, QH, HD), positions).astype(jnp.bfloat16)
    key_heads = key_lin.reshape(TOKENS, HD, KVH).transpose(0, 2, 1)
    rotated_keys = rotate(key_heads, positions).astype(jnp.bfloat16)
    values = value_lin.reshape(TOKENS, HD, KVH).transpose(0, 2, 1)
    group_size = QH // KVH
    attended = attend(queries, jnp.repeat(rotated_keys, group_size, axis=1), jnp.repeat(values, group_size, axis=1), segment_ids)
    head_cols = QH * HD // N_TP
    stacked_in = attended.reshape(TOKENS, N_TP, head_cols).transpose(1, 0, 2)
    stacked_weight = w_out.reshape(N_TP, head_cols, D)

    def add_group(summed, operands):
        part_in, part_weight = operands
        partial_value = jnp.dot(part_in, part_weight, preferred_element_type=jnp.float32)
        part_codes, part_scales = quantize(partial_value)
        return (summed + expand(part_codes, part_scales), None)
    summed, _ = lax.scan(add_group, jnp.zeros((TOKENS, D), jnp.float32), (stacked_in, stacked_weight))
    return residual + summed
```

```python
import functools
import math

import jax
import jax.numpy as jnp
from jax import lax
from jax.experimental import pallas as pl
from jax.experimental.pallas import tpu as pltpu
from jax.sharding import PartitionSpec as P

QH = 64
KVH = 8
HD = 128
BLOCK = 128


code_limit = 448.0
rope_base = 500000.0

NZ, NY, NC = 4, 2, 2
N = NZ * NY * NC
OWN = 4
SUB = 16 // OWN
KC = 4
RC = 8


def one_hot(condition):
    return jnp.where(condition, 1.0, 0.0).astype(jnp.bfloat16)


def token_of_row(row):
    core, y, z, tok = row // 32, (row // 16) % 2, (row // 4) % 4, row % 4
    return ((z * NY + y) * NC + core) * OWN + tok


def dot(a, b):
    return jnp.dot(a, b, preferred_element_type=jnp.float32)


def dot_t(a, b):
    return lax.dot_general(a, b, (((1,), (1,)), ((), ())), preferred_element_type=jnp.float32)


def layer_kernel(
    residual, gain, segments, w_query, w_key, w_value, w_out, out,
    pack, gathered, wq, wkv, wo, q_acc, kv_acc, kv_out, kv_in, attended,
    core_own, core_out, core_in, y_own, y_out, y_in, z_out, z_in, total,
    w_sem, wo_sem, g_recv, g_zsend, g_ysend, g_csend, kv_send, kv_recv,
    c_send, c_recv, y_send, y_recv, z_send, z_recv,
):
    depth = w_query.shape[0]
    chunk = depth // KC
    width = chunk // SUB
    cols = w_out.shape[1] // RC
    quarter = cols // SUB
    tokens = N * OWN
    heads = w_query.shape[1] // HD
    kv_cols = w_key.shape[0]

    me = lax.axis_index("tp")
    z, y, core = me // 4, (me // 2) % 2, me % 2
    y_peer = (z * NY + (1 - y)) * NC + core
    core_peer = (z * NY + y) * NC + (1 - core)

    def at_z(zz):
        return (zz * NY + y) * NC + core

    def weight_copies(k):
        rows = pl.ds(pl.multiple_of(k * chunk, chunk), chunk)
        return [
            pltpu.make_async_copy(w_query.at[rows], wq.at[rows], w_sem.at[0, k]),
            pltpu.make_async_copy(w_key.at[:, rows], wkv.at[k, :kv_cols], w_sem.at[1, k]),
            pltpu.make_async_copy(w_value.at[:, rows], wkv.at[k, kv_cols:], w_sem.at[2, k]),
        ]

    def out_copy(j):
        return pltpu.make_async_copy(
            w_out.at[:, pl.ds(pl.multiple_of(j * cols, cols), cols)], wo.at[j], wo_sem.at[j]
        )

    def remote(src, dst, send, recv, peer):
        return pltpu.make_async_remote_copy(
            src_ref=src, dst_ref=dst, send_sem=send, recv_sem=recv,
            device_id={"tp": peer}, device_id_type=pl.DeviceIdType.MESH,
        )

    def piece_copy(k, src, send, peer):
        return remote(gathered.at[k, src], gathered.at[k, src], send, g_recv.at[k, src], peer)

    def z_copy(k, d):
        return piece_copy(k, me, g_zsend.at[k, d - 1], at_z(lax.rem(z + d, NZ)))

    def y_copy(k, d):
        return piece_copy(k, at_z(lax.rem(z + d, NZ)), g_ysend.at[k, d], y_peer)

    def c_copy(k, d, yy):
        src = (lax.rem(z + d, NZ) * NY + yy) * NC + core
        return piece_copy(k, src, g_csend.at[k, d, yy], core_peer)

    barrier = pltpu.get_barrier_semaphore()

    def greet(d, carry):
        pl.semaphore_signal(
            barrier, inc=1, device_id={"tp": lax.rem(me + d, N)},
            device_id_type=pl.DeviceIdType.MESH,
        )
        return carry

    lax.fori_loop(1, N, greet, 0)
    for k in range(KC):
        for copy in weight_copies(k):
            copy.start()

    values = residual[...]
    inv = lax.rsqrt(jnp.mean(values * values, axis=1, keepdims=True) + 1e-05)
    for k in range(KC):
        for q in range(SUB):
            at = k * chunk + q * width
            pack[k, q * OWN:(q + 1) * OWN, :] = (
                residual[:, at:at + width] * inv * gain[:, at:at + width]
            )
        gathered[k, me] = pack[k].astype(jnp.bfloat16)
    pl.semaphore_wait(barrier, N - 1)

    def send_own(k, carry):
        c_copy(k, 0, y).start()
        y_copy(k, 0).start()
        for d in (1, 2, 3):
            z_copy(k, d).start()
        return carry

    lax.fori_loop(0, KC, send_own, 0)

    q_acc[...] = jnp.zeros_like(q_acc)
    kv_acc[...] = jnp.zeros_like(kv_acc)

    row_i = lax.broadcasted_iota(jnp.int32, (tokens, tokens), 0)
    col_i = lax.broadcasted_iota(jnp.int32, (tokens, tokens), 1)
    row_tok, col_tok = token_of_row(row_i), token_of_row(col_i)
    seg_plain = jnp.broadcast_to(segments[...], (tokens, tokens))
    seg_col = jnp.sum(jnp.where(col_i == row_tok, seg_plain, 0), axis=1, keepdims=True)
    seg_col_plain = jnp.sum(jnp.where(col_i == row_i, seg_plain, 0), axis=1, keepdims=True)
    seg_row = jnp.sum(jnp.where(row_i == col_tok, seg_col_plain, 0), axis=0, keepdims=True)
    start_col = jnp.sum(jnp.where(seg_plain < seg_col, 1, 0), axis=1, keepdims=True)
    start_row = jnp.sum(jnp.where(seg_col_plain < seg_row, 1, 0), axis=0, keepdims=True)
    allowed = (col_tok <= row_tok) & (seg_col == seg_row)
    half = HD // 2
    pos_col = (row_tok[:, :half] - start_col).astype(jnp.float32)
    pos_row = (col_tok[:half, :] - start_row).astype(jnp.float32)
    log_base = math.log(rope_base)
    freq_lane = jnp.exp(col_i[:, :half].astype(jnp.float32) * (-2.0 * log_base / HD))
    freq_row = jnp.exp(row_i[:half, :].astype(jnp.float32) * (-2.0 * log_base / HD))
    cos_q, sin_q = jnp.cos(pos_col * freq_lane), jnp.sin(pos_col * freq_lane)
    cos_k, sin_k = jnp.cos(pos_row * freq_row), jnp.sin(pos_row * freq_row)

    pr = lax.broadcasted_iota(jnp.int32, (N * 16, N * 16), 0)
    pc = lax.broadcasted_iota(jnp.int32, (N * 16, N * 16), 1)
    tok = token_of_row(pr % tokens)
    order = one_hot(pc == (tok // OWN) * 16 + (pr // tokens) * OWN + tok % OWN)

    def gather_step(s, carry):
        @pl.when(s < KC)
        def _():
            for d in (1, 2, 3):
                piece_copy(s, at_z(lax.rem(z + d, NZ)), g_zsend.at[s, 0], y_peer).wait_recv()
                y_copy(s, d).start()
                c_copy(s, d, y).start()

        @pl.when((s >= 1) & (s < KC + 1))
        def _():
            k = s - 1
            for d in range(NZ):
                src = (lax.rem(z + d, NZ) * NY + (1 - y)) * NC + core
                piece_copy(k, src, g_zsend.at[k, 0], y_peer).wait_recv()
                c_copy(k, d, 1 - y).start()
            for copy in weight_copies(k):
                copy.wait()
            for i in range(RC // KC):
                out_copy(k * (RC // KC) + i).start()

        @pl.when(s >= 2)
        def _():
            k = s - 2
            for d in range(N // 2):
                src = d * NC + (1 - core)
                piece_copy(k, src, g_zsend.at[k, 0], y_peer).wait_recv()
            rows = dot(order, gathered[k].reshape(N * 16, width)).astype(jnp.bfloat16)
            for q in range(SUB):
                lhs = rows[q * tokens:(q + 1) * tokens]
                at = pl.ds(pl.multiple_of(k * chunk + q * width, width), width)
                q_acc[...] += dot(lhs, wq[at, :])
                kv_acc[...] += dot_t(wkv[k, :, q * width:(q + 1) * width], lhs)

        return carry

    lax.fori_loop(0, KC + 2, gather_step, 0)

    sr = lax.broadcasted_iota(jnp.int32, (HD, HD), 0)
    sc = lax.broadcasted_iota(jnp.int32, (HD, HD), 1)
    source = ((sr // 8) % 2) * kv_cols + (sr % 8) * KVH + sr // 16
    turned = dot(one_hot(sc == source), kv_acc[...].astype(jnp.bfloat16))
    turned = jnp.concatenate([turned, turned], axis=1).astype(jnp.bfloat16)
    kv_out[...] = turned.reshape(KVH, 16, HD)

    def kv_copy(d):
        peer = lax.rem(me + d, N)
        return remote(kv_out.at[peer // 2], kv_in.at[me], kv_send.at[d], kv_recv.at[me], peer)

    def kv_start(d, carry):
        kv_copy(d).start()
        return carry

    lax.fori_loop(1, N, kv_start, 0)
    kv_in[me] = kv_out[me // 2]

    scale = 1.0 / math.sqrt(HD)
    queries = []
    for h in range(heads):
        lin = q_acc[:, h * HD:(h + 1) * HD].astype(jnp.bfloat16).astype(jnp.float32)
        a, b = lin[:, :half], lin[:, half:]
        queries.append(
            jnp.concatenate([a * cos_q - b * sin_q, b * cos_q + a * sin_q], axis=1)
        )

    def kv_wait(d, carry):
        src = lax.rem(me + d, N)
        remote(kv_out.at[0], kv_in.at[src], kv_send.at[d], kv_recv.at[src], src).wait_recv()
        return carry

    lax.fori_loop(1, N, kv_wait, 0)
    kv = kv_in[...].astype(jnp.float32)
    keys = kv[:, :8, :tokens].reshape(HD, tokens)
    vals = kv[:, 8:, :tokens].reshape(HD, tokens).astype(jnp.bfloat16)
    a, b = keys[:half], keys[half:]
    keys = jnp.concatenate([a * cos_k - b * sin_k, b * cos_k + a * sin_k], axis=0)
    keys = keys.astype(jnp.bfloat16)
    for h in range(heads):
        scores = dot(queries[h].astype(jnp.bfloat16), keys) * scale
        scores = jnp.where(allowed, scores, -1e30)
        weights = jnp.exp(scores - jnp.max(scores, axis=1, keepdims=True))
        probs = (weights / jnp.sum(weights, axis=1, keepdims=True)).astype(jnp.bfloat16)
        attended[:, h * HD:(h + 1) * HD] = dot_t(probs, vals).astype(jnp.bfloat16)

    zr = lax.broadcasted_iota(jnp.int32, (64, 64), 0)
    zc = lax.broadcasted_iota(jnp.int32, (64, 64), 1)
    by_z = one_hot(zc == ((zr // OWN) % SUB) * 16 + (zr // 16) * OWN + zr % OWN)

    def core_copy(j):
        return remote(core_out.at[j], core_in.at[j], c_send.at[j], c_recv.at[j], core_peer)

    def row_copy(j):
        return remote(y_out.at[j], y_in.at[j], y_send.at[j], y_recv.at[j], y_peer)

    def line_copy(j, d):
        zz = lax.rem(z + d, NZ)
        return remote(
            z_out.at[j, zz], z_in.at[j, z], z_send.at[j, d - 1], z_recv.at[j, z], at_z(zz)
        )

    def sum_step(s, carry):
        @pl.when(s < RC)
        def _():
            out_copy(s).wait()
            part = dot(attended[...], wo[s]).reshape(2, 32, cols)
            low, high = part[0], part[1]
            core_out[s] = jnp.where(core == 0, high, low).astype(jnp.bfloat16)
            core_copy(s).start()
            core_own[s] = jnp.where(core == 0, low, high)

        @pl.when((s >= 1) & (s < RC + 1))
        def _():
            j = s - 1
            core_copy(j).wait_recv()
            both = core_own[j] + core_in[j].astype(jnp.float32)
            low, high = both[:16], both[16:]
            y_out[j] = jnp.where(y == 0, high, low).astype(jnp.bfloat16)
            row_copy(j).start()
            y_own[j] = jnp.where(y == 0, low, high)

        @pl.when(s >= 2)
        def _():
            j = s - 2
            row_copy(j).wait_recv()
            both = y_own[j] + y_in[j].astype(jnp.float32)
            stacked = jnp.concatenate(
                [both[:, q * quarter:(q + 1) * quarter] for q in range(SUB)], axis=0
            )
            sorted_rows = dot(by_z, stacked.astype(jnp.bfloat16)).astype(jnp.bfloat16)
            z_out[j] = sorted_rows.reshape(NZ, 16, quarter)
            for d in (1, 2, 3):
                line_copy(j, d).start()

        return carry

    lax.fori_loop(0, RC + 2, sum_step, 0)

    for j in range(RC):
        summed = z_out[j, z].astype(jnp.float32)
        for d in (1, 2, 3):
            zz = lax.rem(z + d, NZ)
            remote(
                z_out.at[j, zz], z_in.at[j, zz], z_send.at[j, 0], z_recv.at[j, zz], at_z(zz)
            ).wait_recv()
            summed = summed + z_in[j, zz].astype(jnp.float32)
        total[j] = summed
        for q in range(SUB):
            at = j * cols + q * quarter
            out[:, at:at + quarter] = total[j, q * OWN:(q + 1) * OWN, :]

    def sent_gather(k, carry):
        for d in range(NZ):
            if d > 0:
                z_copy(k, d).wait_send()
            y_copy(k, d).wait_send()
            c_copy(k, d, 0).wait_send()
            c_copy(k, d, 1).wait_send()
        return carry

    def sent_kv(d, carry):
        kv_copy(d).wait_send()
        return carry

    def sent_sum(j, carry):
        core_copy(j).wait_send()
        row_copy(j).wait_send()
        for d in (1, 2, 3):
            line_copy(j, d).wait_send()
        return carry

    lax.fori_loop(0, KC, sent_gather, 0)
    lax.fori_loop(1, N, sent_kv, 0)
    lax.fori_loop(0, RC, sent_sum, 0)


def per_device_kernel(residual, norm_gain, segment_ids, w_query, w_key, w_value, w_out):
    depth, head_cols = w_query.shape
    kv_cols = w_key.shape[1]
    tokens = segment_ids.shape[0]
    width = depth // KC // SUB
    cols = depth // RC
    quarter = cols // SUB
    f32, bf16 = jnp.float32, jnp.bfloat16
    vmem = pl.BlockSpec(memory_space=pltpu.VMEM)
    hbm = pl.BlockSpec(memory_space=pl.ANY)
    dma = pltpu.SemaphoreType.DMA
    summed = pl.pallas_call(
        layer_kernel,
        out_shape=jax.ShapeDtypeStruct(residual.shape, f32),
        in_specs=[vmem, vmem, vmem, hbm, hbm, hbm, hbm],
        out_specs=vmem,
        scratch_shapes=[
            pltpu.VMEM((KC, 16, width), f32),
            pltpu.VMEM((KC, N, 16, width), bf16),
            pltpu.VMEM((depth, head_cols), bf16),
            pltpu.VMEM((KC, 2 * kv_cols, depth // KC), bf16),
            pltpu.VMEM((RC, head_cols, cols), bf16),
            pltpu.VMEM((tokens, head_cols), f32),
            pltpu.VMEM((2 * kv_cols, tokens), f32),
            pltpu.VMEM((KVH, 16, HD), bf16),
            pltpu.VMEM((N, 16, HD), bf16),
            pltpu.VMEM((tokens, head_cols), bf16),
            pltpu.VMEM((RC, 32, cols), f32),
            pltpu.VMEM((RC, 32, cols), bf16),
            pltpu.VMEM((RC, 32, cols), bf16),
            pltpu.VMEM((RC, 16, cols), f32),
            pltpu.VMEM((RC, 16, cols), bf16),
            pltpu.VMEM((RC, 16, cols), bf16),
            pltpu.VMEM((RC, NZ, 16, quarter), bf16),
            pltpu.VMEM((RC, NZ, 16, quarter), bf16),
            pltpu.VMEM((RC, 16, quarter), f32),
            dma((3, KC)),
            dma((RC,)),
            dma((KC, N)),
            dma((KC, NZ - 1)),
            dma((KC, NZ)),
            dma((KC, NZ, NY)),
            dma((N,)),
            dma((N,)),
            dma((RC,)),
            dma((RC,)),
            dma((RC,)),
            dma((RC,)),
            dma((RC, NZ - 1)),
            dma((RC, NZ)),
        ],
        compiler_params=pltpu.CompilerParams(
            collective_id=0, has_side_effects=True, vmem_limit_bytes=60 * 1024 * 1024
        ),
        name="sublayer",
    )(
        residual, norm_gain.reshape(1, -1), segment_ids.reshape(1, -1),
        w_query, w_key.T, w_value.T, w_out,
    )
    return residual + summed


def quantize(values):
    row_count = values.shape[0]
    blocks = values.reshape(row_count, -1, BLOCK)
    scales = ((jnp.max(jnp.abs(blocks), axis=2) + 1e-06) / code_limit).astype(jnp.bfloat16)
    encoded = (blocks / scales.astype(jnp.float32)[:, :, None]).astype(jnp.bfloat16)
    return (encoded.reshape(row_count, -1), scales)


def expand(encoded, scales):
    row_count = encoded.shape[0]
    blocks = (
        encoded.astype(jnp.float32).reshape(row_count, -1, BLOCK)
        * scales.astype(jnp.float32)[:, :, None]
    )
    return blocks.reshape(row_count, -1)


def positions_of(segment_ids):
    token_count = segment_ids.shape[0]
    token_index = jnp.arange(token_count, dtype=jnp.int32)
    change = jnp.concatenate([jnp.ones((1,), dtype=bool), segment_ids[1:] != segment_ids[:-1]])
    offset = lax.cummax(jnp.where(change, token_index, jnp.zeros_like(token_index)), axis=0)
    return token_index - offset


def rotate(values, positions):
    half_dim = values.shape[-1] // 2
    inv_freq = rope_base ** (-(jnp.arange(half_dim, dtype=jnp.float32) * 2.0) / (2 * half_dim))
    angles = positions.astype(jnp.float32)[:, None] * inv_freq[None, :]
    cosine = jnp.cos(angles)[:, None, :]
    sine_vals = jnp.sin(angles)[:, None, :]
    first_half = values[..., :half_dim].astype(jnp.float32)
    second = values[..., half_dim:].astype(jnp.float32)
    return jnp.concatenate(
        [first_half * cosine - second * sine_vals, second * cosine + first_half * sine_vals],
        axis=-1,
    )


def attend(queries, chosen_keys, chosen_values, segment_ids):
    token_count = queries.shape[0]
    token_index = jnp.arange(token_count, dtype=jnp.int32)
    scores = jnp.einsum(
        "qhd,khd->hqk", queries, chosen_keys, preferred_element_type=jnp.float32
    ) / math.sqrt(queries.shape[2])
    allowed = (token_index[None, :] <= token_index[:, None]) & (
        segment_ids[:, None] == segment_ids[None, :]
    )
    scores = jnp.where(allowed[None], scores, -1e30)
    row_max = jnp.max(scores, axis=2, keepdims=True)
    weights = jnp.exp(scores - row_max)
    probabilities = (weights / jnp.sum(weights, axis=2, keepdims=True)).astype(jnp.bfloat16)
    outputs = jnp.einsum(
        "hqk,khd->qhd", probabilities, chosen_values, preferred_element_type=jnp.float32
    )
    return outputs.astype(jnp.bfloat16).reshape(token_count, -1)


def per_device_general(residual, norm_gain, segment_ids, w_query, w_key, w_value, w_out):
    own_rows = residual.shape[0]
    mean_square = jnp.mean(residual * residual, axis=1, keepdims=True)
    normed = residual * lax.rsqrt(mean_square + 1e-05) * norm_gain[None, :]
    encoded, scales = quantize(normed)
    token_count = segment_ids.shape[0]
    head_cols = w_query.shape[1]
    inputs = expand(
        lax.all_gather(encoded, "tp", axis=0, tiled=True),
        lax.all_gather(scales, "tp", axis=0, tiled=True),
    ).astype(jnp.bfloat16)
    query_part = jnp.dot(inputs, w_query, preferred_element_type=jnp.float32).astype(jnp.bfloat16)
    key_part = jnp.dot(inputs, w_key, preferred_element_type=jnp.float32).astype(jnp.bfloat16)
    value_part = jnp.dot(inputs, w_value, preferred_element_type=jnp.float32).astype(jnp.bfloat16)
    key_lin, value_lin = (
        lax.all_gather(key_part, "tp", axis=1, tiled=True),
        lax.all_gather(value_part, "tp", axis=1, tiled=True),
    )
    positions = positions_of(segment_ids)
    local_heads = head_cols // HD
    queries = rotate(query_part.reshape(token_count, local_heads, HD), positions).astype(
        jnp.bfloat16
    )
    key_heads = key_lin.reshape(token_count, HD, KVH).transpose(0, 2, 1)
    rotated_keys = rotate(key_heads, positions).astype(jnp.bfloat16)
    values = value_lin.reshape(token_count, HD, KVH).transpose(0, 2, 1)
    head_ids = (lax.axis_index("tp") * local_heads + jnp.arange(local_heads, dtype=jnp.int32)) // (
        QH // KVH
    )
    chosen_keys = jnp.take(rotated_keys, head_ids, axis=1)
    chosen_values = jnp.take(values, head_ids, axis=1)
    attended = attend(queries, chosen_keys, chosen_values, segment_ids)
    partial_value = jnp.dot(attended, w_out, preferred_element_type=jnp.float32)
    part_codes, part_scales = quantize(partial_value)
    got_codes, got_scales = (
        lax.all_to_all(part_codes, "tp", split_axis=0, concat_axis=0, tiled=True),
        lax.all_to_all(part_scales, "tp", split_axis=0, concat_axis=0, tiled=True),
    )
    sources = lax.axis_size("tp")
    owner_terms = expand(got_codes, got_scales).reshape(sources, own_rows, -1)
    summed = jnp.sum(owner_terms, axis=0)
    return residual + summed


def solution(mesh):
    in_specs = (
        P(("groups", "tp"), None),
        P(),
        P("groups"),
        P(None, "tp"),
        P(None, "tp"),
        P(None, "tp"),
        P("tp", None),
    )
    out_specs = P(("groups", "tp"), None)
    body = per_device_kernel if mesh.shape["tp"] == N else per_device_general
    return jax.shard_map(
        body, mesh=mesh, in_specs=in_specs, out_specs=out_specs, check_vma=False
    )
```

```python
import functools
import math

import jax
import jax.numpy as jnp
from jax import lax
from jax.experimental import pallas as pl
from jax.experimental.pallas import tpu as pltpu
from jax.sharding import PartitionSpec as P

QH = 64
KVH = 8
HD = 128
BLOCK = 128


code_limit = 448.0
rope_base = 500000.0

NZ, NY, NC = 4, 2, 2
N = NZ * NY * NC
OWN = 4
SUB = 16 // OWN
KC = 4
RC = 8
CORE_LAG, Y_LAG = 2, 4


def one_hot(condition):
    return jnp.where(condition, 1.0, 0.0).astype(jnp.bfloat16)


def token_of_row(row):
    core, y, z, tok = row // 32, (row // 16) % 2, (row // 4) % 4, row % 4
    return ((z * NY + y) * NC + core) * OWN + tok


def dot(a, b):
    return jnp.dot(a, b, preferred_element_type=jnp.float32)


def dot_t(a, b):
    return lax.dot_general(a, b, (((1,), (1,)), ((), ())), preferred_element_type=jnp.float32)


def layer_kernel(
    residual, gain, segments, w_query, w_key, w_value, w_out, out,
    pack, gathered, wq, wkv, wo, q_acc, kv_acc, kv_out, kv_in, attended,
    core_own, core_out, core_in, y_own, y_out, y_in, z_out, z_in, total,
    w_sem, wo_sem, g_recv, g_zsend, g_ysend, g_csend, kv_send, kv_recv,
    c_send, c_recv, y_send, y_recv, z_send, z_recv,
):
    depth = w_query.shape[0]
    chunk = depth // KC
    width = chunk // SUB
    cols = w_out.shape[1] // RC
    quarter = cols // SUB
    tokens = N * OWN
    heads = w_query.shape[1] // HD
    kv_cols = w_key.shape[0]

    me = lax.axis_index("tp")
    z, y, core = me // 4, (me // 2) % 2, me % 2
    y_peer = (z * NY + (1 - y)) * NC + core
    core_peer = (z * NY + y) * NC + (1 - core)

    def at_z(zz):
        return (zz * NY + y) * NC + core

    def weight_copies(k):
        rows = pl.ds(pl.multiple_of(k * chunk, chunk), chunk)
        return [
            pltpu.make_async_copy(w_query.at[rows], wq.at[rows], w_sem.at[0, k]),
            pltpu.make_async_copy(w_key.at[:, rows], wkv.at[k, :kv_cols], w_sem.at[1, k]),
            pltpu.make_async_copy(w_value.at[:, rows], wkv.at[k, kv_cols:], w_sem.at[2, k]),
        ]

    def out_copy(j):
        return pltpu.make_async_copy(
            w_out.at[:, pl.ds(pl.multiple_of(j * cols, cols), cols)], wo.at[j], wo_sem.at[j]
        )

    def remote(src, dst, send, recv, peer):
        return pltpu.make_async_remote_copy(
            src_ref=src, dst_ref=dst, send_sem=send, recv_sem=recv,
            device_id={"tp": peer}, device_id_type=pl.DeviceIdType.MESH,
        )

    def piece_copy(k, src, send, peer):
        return remote(gathered.at[k, src], gathered.at[k, src], send, g_recv.at[k, src], peer)

    def z_copy(k, d):
        return piece_copy(k, me, g_zsend.at[k, d - 1], at_z(lax.rem(z + d, NZ)))

    def y_copy(k, d):
        return piece_copy(k, at_z(lax.rem(z + d, NZ)), g_ysend.at[k, d], y_peer)

    def c_copy(k, d, yy):
        src = (lax.rem(z + d, NZ) * NY + yy) * NC + core
        return piece_copy(k, src, g_csend.at[k, d, yy], core_peer)

    barrier = pltpu.get_barrier_semaphore()

    def greet(d, carry):
        pl.semaphore_signal(
            barrier, inc=1, device_id={"tp": lax.rem(me + d, N)},
            device_id_type=pl.DeviceIdType.MESH,
        )
        return carry

    lax.fori_loop(1, N, greet, 0)
    for k in range(KC):
        for copy in weight_copies(k):
            copy.start()

    values = residual[...]
    inv = lax.rsqrt(jnp.mean(values * values, axis=1, keepdims=True) + 1e-05)
    for k in range(KC):
        for q in range(SUB):
            at = k * chunk + q * width
            pack[k, q * OWN:(q + 1) * OWN, :] = (
                residual[:, at:at + width] * inv * gain[:, at:at + width]
            )
        gathered[k, me] = pack[k].astype(jnp.bfloat16)
    pl.semaphore_wait(barrier, N - 1)

    def send_own(k, carry):
        c_copy(k, 0, y).start()
        y_copy(k, 0).start()
        for d in (1, 2, 3):
            z_copy(k, d).start()
        return carry

    lax.fori_loop(0, KC, send_own, 0)

    q_acc[...] = jnp.zeros_like(q_acc)
    kv_acc[...] = jnp.zeros_like(kv_acc)

    row_i = lax.broadcasted_iota(jnp.int32, (tokens, tokens), 0)
    col_i = lax.broadcasted_iota(jnp.int32, (tokens, tokens), 1)
    row_tok, col_tok = token_of_row(row_i), token_of_row(col_i)
    seg_plain = jnp.broadcast_to(segments[...], (tokens, tokens))
    seg_col = jnp.sum(jnp.where(col_i == row_tok, seg_plain, 0), axis=1, keepdims=True)
    seg_col_plain = jnp.sum(jnp.where(col_i == row_i, seg_plain, 0), axis=1, keepdims=True)
    seg_row = jnp.sum(jnp.where(row_i == col_tok, seg_col_plain, 0), axis=0, keepdims=True)
    start_col = jnp.sum(jnp.where(seg_plain < seg_col, 1, 0), axis=1, keepdims=True)
    start_row = jnp.sum(jnp.where(seg_col_plain < seg_row, 1, 0), axis=0, keepdims=True)
    allowed = (col_tok <= row_tok) & (seg_col == seg_row)
    half = HD // 2
    pos_col = (row_tok[:, :half] - start_col).astype(jnp.float32)
    pos_row = (col_tok[:half, :] - start_row).astype(jnp.float32)
    log_base = math.log(rope_base)
    freq_lane = jnp.exp(col_i[:, :half].astype(jnp.float32) * (-2.0 * log_base / HD))
    freq_row = jnp.exp(row_i[:half, :].astype(jnp.float32) * (-2.0 * log_base / HD))
    cos_q, sin_q = jnp.cos(pos_col * freq_lane), jnp.sin(pos_col * freq_lane)
    cos_k, sin_k = jnp.cos(pos_row * freq_row), jnp.sin(pos_row * freq_row)

    pr = lax.broadcasted_iota(jnp.int32, (N * 16, N * 16), 0)
    pc = lax.broadcasted_iota(jnp.int32, (N * 16, N * 16), 1)
    tok = token_of_row(pr % tokens)
    order = one_hot(pc == (tok // OWN) * 16 + (pr // tokens) * OWN + tok % OWN)

    def gather_step(s, carry):
        @pl.when(s < KC)
        def _():
            for d in (1, 2, 3):
                piece_copy(s, at_z(lax.rem(z + d, NZ)), g_zsend.at[s, 0], y_peer).wait_recv()
                y_copy(s, d).start()
                c_copy(s, d, y).start()

        @pl.when((s >= 1) & (s < KC + 1))
        def _():
            k = s - 1
            for d in range(NZ):
                src = (lax.rem(z + d, NZ) * NY + (1 - y)) * NC + core
                piece_copy(k, src, g_zsend.at[k, 0], y_peer).wait_recv()
                c_copy(k, d, 1 - y).start()
            for copy in weight_copies(k):
                copy.wait()
            for i in range(RC // KC):
                out_copy(k * (RC // KC) + i).start()

        @pl.when(s >= 2)
        def _():
            k = s - 2
            for d in range(N // 2):
                src = d * NC + (1 - core)
                piece_copy(k, src, g_zsend.at[k, 0], y_peer).wait_recv()
            rows = dot(order, gathered[k].reshape(N * 16, width)).astype(jnp.bfloat16)
            for q in range(SUB):
                lhs = rows[q * tokens:(q + 1) * tokens]
                at = pl.ds(pl.multiple_of(k * chunk + q * width, width), width)
                q_acc[...] += dot(lhs, wq[at, :])
                kv_acc[...] += dot_t(wkv[k, :, q * width:(q + 1) * width], lhs)

        return carry

    lax.fori_loop(0, KC + 2, gather_step, 0)

    sr = lax.broadcasted_iota(jnp.int32, (HD, HD), 0)
    sc = lax.broadcasted_iota(jnp.int32, (HD, HD), 1)
    source = ((sr // 8) % 2) * kv_cols + (sr % 8) * KVH + sr // 16
    turned = dot(one_hot(sc == source), kv_acc[...].astype(jnp.bfloat16))
    turned = jnp.concatenate([turned, turned], axis=1).astype(jnp.bfloat16)
    kv_out[...] = turned.reshape(KVH, 16, HD)

    def kv_copy(d):
        peer = lax.rem(me + d, N)
        return remote(kv_out.at[peer // 2], kv_in.at[me], kv_send.at[d], kv_recv.at[me], peer)

    def kv_start(d, carry):
        kv_copy(d).start()
        return carry

    lax.fori_loop(1, N, kv_start, 0)
    kv_in[me] = kv_out[me // 2]

    scale = 1.0 / math.sqrt(HD)
    queries = []
    for h in range(heads):
        lin = q_acc[:, h * HD:(h + 1) * HD].astype(jnp.bfloat16).astype(jnp.float32)
        a, b = lin[:, :half], lin[:, half:]
        queries.append(
            jnp.concatenate([a * cos_q - b * sin_q, b * cos_q + a * sin_q], axis=1)
        )

    def kv_wait(d, carry):
        src = lax.rem(me + d, N)
        remote(kv_out.at[0], kv_in.at[src], kv_send.at[d], kv_recv.at[src], src).wait_recv()
        return carry

    lax.fori_loop(1, N, kv_wait, 0)
    kv = kv_in[...].astype(jnp.float32)
    keys = kv[:, :8, :tokens].reshape(HD, tokens)
    vals = kv[:, 8:, :tokens].reshape(HD, tokens).astype(jnp.bfloat16)
    a, b = keys[:half], keys[half:]
    keys = jnp.concatenate([a * cos_k - b * sin_k, b * cos_k + a * sin_k], axis=0)
    keys = keys.astype(jnp.bfloat16)
    for h in range(heads):
        scores = dot(queries[h].astype(jnp.bfloat16), keys) * scale
        scores = jnp.where(allowed, scores, -1e30)
        weights = jnp.exp(scores - jnp.max(scores, axis=1, keepdims=True))
        probs = (weights / jnp.sum(weights, axis=1, keepdims=True)).astype(jnp.bfloat16)
        attended[:, h * HD:(h + 1) * HD] = dot_t(probs, vals).astype(jnp.bfloat16)

    zr = lax.broadcasted_iota(jnp.int32, (64, 64), 0)
    zc = lax.broadcasted_iota(jnp.int32, (64, 64), 1)
    by_z = one_hot(zc == ((zr // OWN) % SUB) * 16 + (zr // 16) * OWN + zr % OWN)

    def core_copy(j):
        return remote(core_out.at[j], core_in.at[j], c_send.at[j], c_recv.at[j], core_peer)

    def row_copy(j):
        return remote(y_out.at[j], y_in.at[j], y_send.at[j], y_recv.at[j], y_peer)

    def line_copy(j, d):
        zz = lax.rem(z + d, NZ)
        return remote(
            z_out.at[j, zz], z_in.at[j, z], z_send.at[j, d - 1], z_recv.at[j, z], at_z(zz)
        )

    def sum_step(s, carry):
        @pl.when(s < RC)
        def _():
            out_copy(s).wait()
            part = dot(attended[...], wo[s]).reshape(2, 32, cols)
            low, high = part[0], part[1]
            core_out[s] = jnp.where(core == 0, high, low).astype(jnp.bfloat16)
            core_copy(s).start()
            core_own[s] = jnp.where(core == 0, low, high)

        @pl.when((s >= CORE_LAG) & (s < RC + CORE_LAG))
        def _():
            j = s - CORE_LAG
            core_copy(j).wait_recv()
            both = core_own[j] + core_in[j].astype(jnp.float32)
            low, high = both[:16], both[16:]
            y_out[j] = jnp.where(y == 0, high, low).astype(jnp.bfloat16)
            row_copy(j).start()
            y_own[j] = jnp.where(y == 0, low, high)

        @pl.when(s >= Y_LAG)
        def _():
            j = s - Y_LAG
            row_copy(j).wait_recv()
            both = y_own[j] + y_in[j].astype(jnp.float32)
            stacked = jnp.concatenate(
                [both[:, q * quarter:(q + 1) * quarter] for q in range(SUB)], axis=0
            )
            sorted_rows = dot(by_z, stacked.astype(jnp.bfloat16)).astype(jnp.bfloat16)
            z_out[j] = sorted_rows.reshape(NZ, 16, quarter)
            for d in (1, 2, 3):
                line_copy(j, d).start()

        return carry

    lax.fori_loop(0, RC + Y_LAG, sum_step, 0)

    for j in range(RC):
        summed = z_out[j, z].astype(jnp.float32)
        for d in (1, 2, 3):
            zz = lax.rem(z + d, NZ)
            remote(
                z_out.at[j, zz], z_in.at[j, zz], z_send.at[j, 0], z_recv.at[j, zz], at_z(zz)
            ).wait_recv()
            summed = summed + z_in[j, zz].astype(jnp.float32)
        total[j] = summed
        for q in range(SUB):
            at = j * cols + q * quarter
            out[:, at:at + quarter] = total[j, q * OWN:(q + 1) * OWN, :]

    def sent_gather(k, carry):
        for d in range(NZ):
            if d > 0:
                z_copy(k, d).wait_send()
            y_copy(k, d).wait_send()
            c_copy(k, d, 0).wait_send()
            c_copy(k, d, 1).wait_send()
        return carry

    def sent_kv(d, carry):
        kv_copy(d).wait_send()
        return carry

    def sent_sum(j, carry):
        core_copy(j).wait_send()
        row_copy(j).wait_send()
        for d in (1, 2, 3):
            line_copy(j, d).wait_send()
        return carry

    lax.fori_loop(0, KC, sent_gather, 0)
    lax.fori_loop(1, N, sent_kv, 0)
    lax.fori_loop(0, RC, sent_sum, 0)


def per_device_kernel(residual, norm_gain, segment_ids, w_query, w_key, w_value, w_out):
    depth, head_cols = w_query.shape
    kv_cols = w_key.shape[1]
    tokens = segment_ids.shape[0]
    width = depth // KC // SUB
    cols = depth // RC
    quarter = cols // SUB
    f32, bf16 = jnp.float32, jnp.bfloat16
    vmem = pl.BlockSpec(memory_space=pltpu.VMEM)
    hbm = pl.BlockSpec(memory_space=pl.ANY)
    dma = pltpu.SemaphoreType.DMA
    summed = pl.pallas_call(
        layer_kernel,
        out_shape=jax.ShapeDtypeStruct(residual.shape, f32),
        in_specs=[vmem, vmem, vmem, hbm, hbm, hbm, hbm],
        out_specs=vmem,
        scratch_shapes=[
            pltpu.VMEM((KC, 16, width), f32),
            pltpu.VMEM((KC, N, 16, width), bf16),
            pltpu.VMEM((depth, head_cols), bf16),
            pltpu.VMEM((KC, 2 * kv_cols, depth // KC), bf16),
            pltpu.VMEM((RC, head_cols, cols), bf16),
            pltpu.VMEM((tokens, head_cols), f32),
            pltpu.VMEM((2 * kv_cols, tokens), f32),
            pltpu.VMEM((KVH, 16, HD), bf16),
            pltpu.VMEM((N, 16, HD), bf16),
            pltpu.VMEM((tokens, head_cols), bf16),
            pltpu.VMEM((RC, 32, cols), f32),
            pltpu.VMEM((RC, 32, cols), bf16),
            pltpu.VMEM((RC, 32, cols), bf16),
            pltpu.VMEM((RC, 16, cols), f32),
            pltpu.VMEM((RC, 16, cols), bf16),
            pltpu.VMEM((RC, 16, cols), bf16),
            pltpu.VMEM((RC, NZ, 16, quarter), bf16),
            pltpu.VMEM((RC, NZ, 16, quarter), bf16),
            pltpu.VMEM((RC, 16, quarter), f32),
            dma((3, KC)),
            dma((RC,)),
            dma((KC, N)),
            dma((KC, NZ - 1)),
            dma((KC, NZ)),
            dma((KC, NZ, NY)),
            dma((N,)),
            dma((N,)),
            dma((RC,)),
            dma((RC,)),
            dma((RC,)),
            dma((RC,)),
            dma((RC, NZ - 1)),
            dma((RC, NZ)),
        ],
        compiler_params=pltpu.CompilerParams(
            collective_id=0, has_side_effects=True, vmem_limit_bytes=60 * 1024 * 1024
        ),
        name="sublayer",
    )(
        residual, norm_gain.reshape(1, -1), segment_ids.reshape(1, -1),
        w_query, w_key.T, w_value.T, w_out,
    )
    return residual + summed


def quantize(values):
    row_count = values.shape[0]
    blocks = values.reshape(row_count, -1, BLOCK)
    scales = ((jnp.max(jnp.abs(blocks), axis=2) + 1e-06) / code_limit).astype(jnp.bfloat16)
    encoded = (blocks / scales.astype(jnp.float32)[:, :, None]).astype(jnp.bfloat16)
    return (encoded.reshape(row_count, -1), scales)


def expand(encoded, scales):
    row_count = encoded.shape[0]
    blocks = (
        encoded.astype(jnp.float32).reshape(row_count, -1, BLOCK)
        * scales.astype(jnp.float32)[:, :, None]
    )
    return blocks.reshape(row_count, -1)


def positions_of(segment_ids):
    token_count = segment_ids.shape[0]
    token_index = jnp.arange(token_count, dtype=jnp.int32)
    change = jnp.concatenate([jnp.ones((1,), dtype=bool), segment_ids[1:] != segment_ids[:-1]])
    offset = lax.cummax(jnp.where(change, token_index, jnp.zeros_like(token_index)), axis=0)
    return token_index - offset


def rotate(values, positions):
    half_dim = values.shape[-1] // 2
    inv_freq = rope_base ** (-(jnp.arange(half_dim, dtype=jnp.float32) * 2.0) / (2 * half_dim))
    angles = positions.astype(jnp.float32)[:, None] * inv_freq[None, :]
    cosine = jnp.cos(angles)[:, None, :]
    sine_vals = jnp.sin(angles)[:, None, :]
    first_half = values[..., :half_dim].astype(jnp.float32)
    second = values[..., half_dim:].astype(jnp.float32)
    return jnp.concatenate(
        [first_half * cosine - second * sine_vals, second * cosine + first_half * sine_vals],
        axis=-1,
    )


def attend(queries, chosen_keys, chosen_values, segment_ids):
    token_count = queries.shape[0]
    token_index = jnp.arange(token_count, dtype=jnp.int32)
    scores = jnp.einsum(
        "qhd,khd->hqk", queries, chosen_keys, preferred_element_type=jnp.float32
    ) / math.sqrt(queries.shape[2])
    allowed = (token_index[None, :] <= token_index[:, None]) & (
        segment_ids[:, None] == segment_ids[None, :]
    )
    scores = jnp.where(allowed[None], scores, -1e30)
    row_max = jnp.max(scores, axis=2, keepdims=True)
    weights = jnp.exp(scores - row_max)
    probabilities = (weights / jnp.sum(weights, axis=2, keepdims=True)).astype(jnp.bfloat16)
    outputs = jnp.einsum(
        "hqk,khd->qhd", probabilities, chosen_values, preferred_element_type=jnp.float32
    )
    return outputs.astype(jnp.bfloat16).reshape(token_count, -1)


def per_device_general(residual, norm_gain, segment_ids, w_query, w_key, w_value, w_out):
    own_rows = residual.shape[0]
    mean_square = jnp.mean(residual * residual, axis=1, keepdims=True)
    normed = residual * lax.rsqrt(mean_square + 1e-05) * norm_gain[None, :]
    encoded, scales = quantize(normed)
    token_count = segment_ids.shape[0]
    head_cols = w_query.shape[1]
    inputs = expand(
        lax.all_gather(encoded, "tp", axis=0, tiled=True),
        lax.all_gather(scales, "tp", axis=0, tiled=True),
    ).astype(jnp.bfloat16)
    query_part = jnp.dot(inputs, w_query, preferred_element_type=jnp.float32).astype(jnp.bfloat16)
    key_part = jnp.dot(inputs, w_key, preferred_element_type=jnp.float32).astype(jnp.bfloat16)
    value_part = jnp.dot(inputs, w_value, preferred_element_type=jnp.float32).astype(jnp.bfloat16)
    key_lin, value_lin = (
        lax.all_gather(key_part, "tp", axis=1, tiled=True),
        lax.all_gather(value_part, "tp", axis=1, tiled=True),
    )
    positions = positions_of(segment_ids)
    local_heads = head_cols // HD
    queries = rotate(query_part.reshape(token_count, local_heads, HD), positions).astype(
        jnp.bfloat16
    )
    key_heads = key_lin.reshape(token_count, HD, KVH).transpose(0, 2, 1)
    rotated_keys = rotate(key_heads, positions).astype(jnp.bfloat16)
    values = value_lin.reshape(token_count, HD, KVH).transpose(0, 2, 1)
    head_ids = (lax.axis_index("tp") * local_heads + jnp.arange(local_heads, dtype=jnp.int32)) // (
        QH // KVH
    )
    chosen_keys = jnp.take(rotated_keys, head_ids, axis=1)
    chosen_values = jnp.take(values, head_ids, axis=1)
    attended = attend(queries, chosen_keys, chosen_values, segment_ids)
    partial_value = jnp.dot(attended, w_out, preferred_element_type=jnp.float32)
    part_codes, part_scales = quantize(partial_value)
    got_codes, got_scales = (
        lax.all_to_all(part_codes, "tp", split_axis=0, concat_axis=0, tiled=True),
        lax.all_to_all(part_scales, "tp", split_axis=0, concat_axis=0, tiled=True),
    )
    sources = lax.axis_size("tp")
    owner_terms = expand(got_codes, got_scales).reshape(sources, own_rows, -1)
    summed = jnp.sum(owner_terms, axis=0)
    return residual + summed


def solution(mesh):
    in_specs = (
        P(("groups", "tp"), None),
        P(),
        P("groups"),
        P(None, "tp"),
        P(None, "tp"),
        P(None, "tp"),
        P("tp", None),
    )
    out_specs = P(("groups", "tp"), None)
    body = per_device_kernel if mesh.shape["tp"] == N else per_device_general
    return jax.shard_map(
        body, mesh=mesh, in_specs=in_specs, out_specs=out_specs, check_vma=False
    )
```

```python
import functools
import math

import jax
import jax.numpy as jnp
from jax import lax
from jax.experimental import pallas as pl
from jax.experimental.pallas import tpu as pltpu
from jax.sharding import PartitionSpec as P

QH = 64
KVH = 8
HD = 128
BLOCK = 128


code_limit = 448.0
rope_base = 500000.0

NZ, NY, NC = 4, 2, 2
N = NZ * NY * NC
OWN = 4
SUB = 16 // OWN
KC = 4
RC = 8
CORE_LAG, Y_LAG, Z_LAG = 2, 4, 7


def one_hot(condition):
    return jnp.where(condition, 1.0, 0.0).astype(jnp.bfloat16)


def token_of_row(row):
    core, y, z, tok = row // 32, (row // 16) % 2, (row // 4) % 4, row % 4
    return ((z * NY + y) * NC + core) * OWN + tok


def dot(a, b):
    return jnp.dot(a, b, preferred_element_type=jnp.float32)


def dot_t(a, b):
    return lax.dot_general(a, b, (((1,), (1,)), ((), ())), preferred_element_type=jnp.float32)


def layer_kernel(
    residual, gain, segments, w_query, w_key, w_value, w_out, out,
    pack, gathered, wq, wkv, wo, q_acc, kv_acc, kv_out, kv_in, attended,
    core_own, core_out, core_in, y_own, y_out, y_in, z_out, z_in, total,
    w_sem, wo_sem, g_recv, g_zsend, g_ysend, g_csend, kv_send, kv_recv,
    c_send, c_recv, y_send, y_recv, z_send, z_recv,
):
    depth = w_query.shape[0]
    chunk = depth // KC
    width = chunk // SUB
    cols = w_out.shape[1] // RC
    quarter = cols // SUB
    tokens = N * OWN
    heads = w_query.shape[1] // HD
    kv_cols = w_key.shape[0]

    me = lax.axis_index("tp")
    z, y, core = me // 4, (me // 2) % 2, me % 2
    y_peer = (z * NY + (1 - y)) * NC + core
    core_peer = (z * NY + y) * NC + (1 - core)

    def at_z(zz):
        return (zz * NY + y) * NC + core

    def weight_copies(k):
        rows = pl.ds(pl.multiple_of(k * chunk, chunk), chunk)
        return [
            pltpu.make_async_copy(w_query.at[rows], wq.at[rows], w_sem.at[0, k]),
            pltpu.make_async_copy(w_key.at[:, rows], wkv.at[k, :kv_cols], w_sem.at[1, k]),
            pltpu.make_async_copy(w_value.at[:, rows], wkv.at[k, kv_cols:], w_sem.at[2, k]),
        ]

    def out_copy(j):
        return pltpu.make_async_copy(
            w_out.at[:, pl.ds(pl.multiple_of(j * cols, cols), cols)], wo.at[j], wo_sem.at[j]
        )

    def remote(src, dst, send, recv, peer):
        return pltpu.make_async_remote_copy(
            src_ref=src, dst_ref=dst, send_sem=send, recv_sem=recv,
            device_id={"tp": peer}, device_id_type=pl.DeviceIdType.MESH,
        )

    def piece_copy(k, src, send, peer):
        return remote(gathered.at[k, src], gathered.at[k, src], send, g_recv.at[k, src], peer)

    def z_copy(k, d):
        return piece_copy(k, me, g_zsend.at[k, d - 1], at_z(lax.rem(z + d, NZ)))

    def near_line(d):
        return jnp.logical_not(
            ((z == 0) & (d == NZ - 1)) | ((z == NZ - 1) & (d == 1))
        )

    inner = (z == 1) | (z == 2)
    far = jnp.where(z == 1, NZ - 1, 0)
    beyond = jnp.where(z == 1, 0, NZ - 1)

    def relay_copy(k):
        return piece_copy(k, at_z(far), g_zsend.at[k, NZ - 1], at_z(beyond))

    def y_copy(k, d):
        return piece_copy(k, at_z(lax.rem(z + d, NZ)), g_ysend.at[k, d], y_peer)

    def c_copy(k, d, yy):
        src = (lax.rem(z + d, NZ) * NY + yy) * NC + core
        return piece_copy(k, src, g_csend.at[k, d, yy], core_peer)

    barrier = pltpu.get_barrier_semaphore()

    line = [at_z(lax.rem(z + d, NZ)) for d in range(1, NZ)]
    for peer in [y_peer, core_peer] + line:
        pl.semaphore_signal(
            barrier, inc=1, device_id={"tp": peer}, device_id_type=pl.DeviceIdType.MESH
        )
    for k in range(KC):
        for copy in weight_copies(k):
            copy.start()

    values = residual[...]
    inv = lax.rsqrt(jnp.mean(values * values, axis=1, keepdims=True) + 1e-05)
    for k in range(KC):
        for q in range(SUB):
            at = k * chunk + q * width
            pack[k, q * OWN:(q + 1) * OWN, :] = (
                residual[:, at:at + width] * inv * gain[:, at:at + width]
            )
        gathered[k, me] = pack[k].astype(jnp.bfloat16)
    pl.semaphore_wait(barrier, NZ + 1)

    def send_own(k, carry):
        c_copy(k, 0, y).start()
        y_copy(k, 0).start()
        for d in (1, 2, 3):
            pl.when(near_line(d))(lambda: z_copy(k, d).start())
        return carry

    lax.fori_loop(0, KC, send_own, 0)

    q_acc[...] = jnp.zeros_like(q_acc)
    kv_acc[...] = jnp.zeros_like(kv_acc)

    row_i = lax.broadcasted_iota(jnp.int32, (tokens, tokens), 0)
    col_i = lax.broadcasted_iota(jnp.int32, (tokens, tokens), 1)
    row_tok, col_tok = token_of_row(row_i), token_of_row(col_i)
    seg_plain = jnp.broadcast_to(segments[...], (tokens, tokens))
    seg_col = jnp.sum(jnp.where(col_i == row_tok, seg_plain, 0), axis=1, keepdims=True)
    seg_col_plain = jnp.sum(jnp.where(col_i == row_i, seg_plain, 0), axis=1, keepdims=True)
    seg_row = jnp.sum(jnp.where(row_i == col_tok, seg_col_plain, 0), axis=0, keepdims=True)
    start_col = jnp.sum(jnp.where(seg_plain < seg_col, 1, 0), axis=1, keepdims=True)
    start_row = jnp.sum(jnp.where(seg_col_plain < seg_row, 1, 0), axis=0, keepdims=True)
    allowed = (col_tok <= row_tok) & (seg_col == seg_row)
    half = HD // 2
    pos_col = (row_tok[:, :half] - start_col).astype(jnp.float32)
    pos_row = (col_tok[:half, :] - start_row).astype(jnp.float32)
    log_base = math.log(rope_base)
    freq_lane = jnp.exp(col_i[:, :half].astype(jnp.float32) * (-2.0 * log_base / HD))
    freq_row = jnp.exp(row_i[:half, :].astype(jnp.float32) * (-2.0 * log_base / HD))
    cos_q, sin_q = jnp.cos(pos_col * freq_lane), jnp.sin(pos_col * freq_lane)
    cos_k, sin_k = jnp.cos(pos_row * freq_row), jnp.sin(pos_row * freq_row)

    pr = lax.broadcasted_iota(jnp.int32, (N * 16, N * 16), 0)
    pc = lax.broadcasted_iota(jnp.int32, (N * 16, N * 16), 1)
    tok = token_of_row(pr % tokens)
    order = one_hot(pc == (tok // OWN) * 16 + (pr // tokens) * OWN + tok % OWN)

    def gather_step(s, carry):
        @pl.when(s < KC)
        def _():
            order_z = (
                jnp.where(z == 0, 1, z - 1),
                jnp.where(z == 3, 1, jnp.where(z == 2, 3, 2)),
                jnp.where(z < 2, 3, 0),
            )
            for i, zz in enumerate(order_z):
                d = lax.rem(zz - z + NZ, NZ)
                piece_copy(s, at_z(zz), g_zsend.at[s, 0], y_peer).wait_recv()
                if i == 2:
                    pl.when(inner)(lambda: relay_copy(s).start())
                y_copy(s, d).start()
                c_copy(s, d, y).start()

        @pl.when((s >= 1) & (s < KC + 1))
        def _():
            k = s - 1
            for d in range(NZ):
                src = (lax.rem(z + d, NZ) * NY + (1 - y)) * NC + core
                piece_copy(k, src, g_zsend.at[k, 0], y_peer).wait_recv()
                c_copy(k, d, 1 - y).start()
            for copy in weight_copies(k):
                copy.wait()
            for i in range(RC // KC):
                out_copy(k * (RC // KC) + i).start()

        @pl.when(s >= 2)
        def _():
            k = s - 2
            rows = sorted_rows(k)
            add_keys(k, rows)
            add_queries(k, rows)

        return carry

    def sorted_rows(k):
        for d in range(N // 2):
            src = d * NC + (1 - core)
            piece_copy(k, src, g_zsend.at[k, 0], y_peer).wait_recv()
        return dot(order, gathered[k].reshape(N * 16, width)).astype(jnp.bfloat16)

    def add_keys(k, rows):
        for q in range(SUB):
            lhs = rows[q * tokens:(q + 1) * tokens]
            kv_acc[...] += dot_t(wkv[k, :, q * width:(q + 1) * width], lhs)

    def add_queries(k, rows):
        for q in range(SUB):
            lhs = rows[q * tokens:(q + 1) * tokens]
            at = pl.ds(pl.multiple_of(k * chunk + q * width, width), width)
            q_acc[...] += dot(lhs, wq[at, :])

    lax.fori_loop(0, KC + 1, gather_step, 0)
    last_rows = sorted_rows(KC - 1)
    add_keys(KC - 1, last_rows)

    sr = lax.broadcasted_iota(jnp.int32, (HD, HD), 0)
    sc = lax.broadcasted_iota(jnp.int32, (HD, HD), 1)
    source = ((sr // 8) % 2) * kv_cols + (sr % 8) * KVH + sr // 16
    turned = dot(one_hot(sc == source), kv_acc[...].astype(jnp.bfloat16))
    turned = jnp.concatenate([turned, turned], axis=1).astype(jnp.bfloat16)
    kv_out[...] = turned.reshape(KVH, 16, HD)

    def kv_copy(d):
        peer = lax.rem(me + d, N)
        return remote(kv_out.at[peer // 2], kv_in.at[me], kv_send.at[d], kv_recv.at[me], peer)

    def kv_start(d, carry):
        kv_copy(d).start()
        return carry

    lax.fori_loop(1, N, kv_start, 0)
    kv_in[me] = kv_out[me // 2]
    add_queries(KC - 1, last_rows)

    scale = 1.0 / math.sqrt(HD)
    queries = []
    for h in range(heads):
        lin = q_acc[:, h * HD:(h + 1) * HD].astype(jnp.bfloat16).astype(jnp.float32)
        a, b = lin[:, :half], lin[:, half:]
        queries.append(
            jnp.concatenate([a * cos_q - b * sin_q, b * cos_q + a * sin_q], axis=1)
        )

    def kv_wait(d, carry):
        src = lax.rem(me + d, N)
        remote(kv_out.at[0], kv_in.at[src], kv_send.at[d], kv_recv.at[src], src).wait_recv()
        return carry

    lax.fori_loop(1, N, kv_wait, 0)
    kv = kv_in[...].astype(jnp.float32)
    keys = kv[:, :8, :tokens].reshape(HD, tokens)
    vals = kv[:, 8:, :tokens].reshape(HD, tokens).astype(jnp.bfloat16)
    a, b = keys[:half], keys[half:]
    keys = jnp.concatenate([a * cos_k - b * sin_k, b * cos_k + a * sin_k], axis=0)
    keys = keys.astype(jnp.bfloat16)
    stacked = jnp.concatenate(queries, axis=0).astype(jnp.bfloat16)
    scores = dot(stacked, keys) * scale
    scores = jnp.where(jnp.concatenate([allowed] * heads, axis=0), scores, -1e30)
    weights = jnp.exp(scores - jnp.max(scores, axis=1, keepdims=True))
    probs = (weights / jnp.sum(weights, axis=1, keepdims=True)).astype(jnp.bfloat16)
    mixed = dot_t(probs, vals).astype(jnp.bfloat16)
    for h in range(heads):
        attended[:, h * HD:(h + 1) * HD] = mixed[h * tokens:(h + 1) * tokens]

    zr = lax.broadcasted_iota(jnp.int32, (64, 64), 0)
    zc = lax.broadcasted_iota(jnp.int32, (64, 64), 1)
    by_z = one_hot(zc == ((zr // OWN) % SUB) * 16 + (zr // 16) * OWN + zr % OWN)

    def core_copy(j):
        return remote(core_out.at[j], core_in.at[j], c_send.at[j], c_recv.at[j], core_peer)

    def row_copy(j):
        return remote(y_out.at[j], y_in.at[j], y_send.at[j], y_recv.at[j], y_peer)

    def line_copy(j, d):
        zz = lax.rem(z + d, NZ)
        return remote(
            z_out.at[j, zz], z_in.at[j, z], z_send.at[j, d - 1], z_recv.at[j, z], at_z(zz)
        )

    def sum_step(s, carry):
        @pl.when(s < RC)
        def _():
            out_copy(s).wait()
            part = dot(attended[...], wo[s]).reshape(2, 32, cols)
            low, high = part[0], part[1]
            core_out[s] = jnp.where(core == 0, high, low).astype(jnp.bfloat16)
            core_copy(s).start()
            core_own[s] = jnp.where(core == 0, low, high)

        @pl.when((s >= CORE_LAG) & (s < RC + CORE_LAG))
        def _():
            j = s - CORE_LAG
            core_copy(j).wait_recv()
            both = core_own[j] + core_in[j].astype(jnp.float32)
            low, high = both[:16], both[16:]
            y_out[j] = jnp.where(y == 0, high, low).astype(jnp.bfloat16)
            row_copy(j).start()
            y_own[j] = jnp.where(y == 0, low, high)

        @pl.when((s >= Y_LAG) & (s < RC + Y_LAG))
        def _():
            j = s - Y_LAG
            row_copy(j).wait_recv()
            both = y_own[j] + y_in[j].astype(jnp.float32)
            stacked = jnp.concatenate(
                [both[:, q * quarter:(q + 1) * quarter] for q in range(SUB)], axis=0
            )
            sorted_rows = dot(by_z, stacked.astype(jnp.bfloat16)).astype(jnp.bfloat16)
            z_out[j] = sorted_rows.reshape(NZ, 16, quarter)
            for d in (1, 2, 3):
                line_copy(j, d).start()

        @pl.when(s >= Z_LAG)
        def _():
            j = s - Z_LAG
            summed = z_out[j, z].astype(jnp.float32)
            for d in (1, 2, 3):
                zz = lax.rem(z + d, NZ)
                remote(
                    z_out.at[j, zz], z_in.at[j, zz], z_send.at[j, 0], z_recv.at[j, zz], at_z(zz)
                ).wait_recv()
                summed = summed + z_in[j, zz].astype(jnp.float32)
            total[j] = summed
            for q in range(SUB):
                at = pl.ds(pl.multiple_of(j * cols + q * quarter, quarter), quarter)
                out[:, at] = total[j, q * OWN:(q + 1) * OWN, :]

        return carry

    lax.fori_loop(0, RC + Z_LAG, sum_step, 0)

    def sent_gather(k, carry):
        pl.when(inner)(lambda: relay_copy(k).wait_send())
        for d in range(NZ):
            if d > 0:
                pl.when(near_line(d))(lambda: z_copy(k, d).wait_send())
            y_copy(k, d).wait_send()
            c_copy(k, d, 0).wait_send()
            c_copy(k, d, 1).wait_send()
        return carry

    def sent_kv(d, carry):
        kv_copy(d).wait_send()
        return carry

    def sent_sum(j, carry):
        core_copy(j).wait_send()
        row_copy(j).wait_send()
        for d in (1, 2, 3):
            line_copy(j, d).wait_send()
        return carry

    lax.fori_loop(0, KC, sent_gather, 0)
    lax.fori_loop(1, N, sent_kv, 0)
    lax.fori_loop(0, RC, sent_sum, 0)


def per_device_kernel(residual, norm_gain, segment_ids, w_query, w_key, w_value, w_out):
    depth, head_cols = w_query.shape
    kv_cols = w_key.shape[1]
    tokens = segment_ids.shape[0]
    width = depth // KC // SUB
    cols = depth // RC
    quarter = cols // SUB
    f32, bf16 = jnp.float32, jnp.bfloat16
    vmem = pl.BlockSpec(memory_space=pltpu.VMEM)
    hbm = pl.BlockSpec(memory_space=pl.ANY)
    dma = pltpu.SemaphoreType.DMA
    summed = pl.pallas_call(
        layer_kernel,
        out_shape=jax.ShapeDtypeStruct(residual.shape, f32),
        in_specs=[vmem, vmem, vmem, hbm, hbm, hbm, hbm],
        out_specs=vmem,
        scratch_shapes=[
            pltpu.VMEM((KC, 16, width), f32),
            pltpu.VMEM((KC, N, 16, width), bf16),
            pltpu.VMEM((depth, head_cols), bf16),
            pltpu.VMEM((KC, 2 * kv_cols, depth // KC), bf16),
            pltpu.VMEM((RC, head_cols, cols), bf16),
            pltpu.VMEM((tokens, head_cols), f32),
            pltpu.VMEM((2 * kv_cols, tokens), f32),
            pltpu.VMEM((KVH, 16, HD), bf16),
            pltpu.VMEM((N, 16, HD), bf16),
            pltpu.VMEM((tokens, head_cols), bf16),
            pltpu.VMEM((RC, 32, cols), f32),
            pltpu.VMEM((RC, 32, cols), bf16),
            pltpu.VMEM((RC, 32, cols), bf16),
            pltpu.VMEM((RC, 16, cols), f32),
            pltpu.VMEM((RC, 16, cols), bf16),
            pltpu.VMEM((RC, 16, cols), bf16),
            pltpu.VMEM((RC, NZ, 16, quarter), bf16),
            pltpu.VMEM((RC, NZ, 16, quarter), bf16),
            pltpu.VMEM((RC, 16, quarter), f32),
            dma((3, KC)),
            dma((RC,)),
            dma((KC, N)),
            dma((KC, NZ)),
            dma((KC, NZ)),
            dma((KC, NZ, NY)),
            dma((N,)),
            dma((N,)),
            dma((RC,)),
            dma((RC,)),
            dma((RC,)),
            dma((RC,)),
            dma((RC, NZ - 1)),
            dma((RC, NZ)),
        ],
        compiler_params=pltpu.CompilerParams(
            collective_id=0, has_side_effects=True, vmem_limit_bytes=60 * 1024 * 1024
        ),
        name="sublayer",
    )(
        residual, norm_gain.reshape(1, -1), segment_ids.reshape(1, -1),
        w_query, w_key.T, w_value.T, w_out,
    )
    return residual + summed


def quantize(values):
    row_count = values.shape[0]
    blocks = values.reshape(row_count, -1, BLOCK)
    scales = ((jnp.max(jnp.abs(blocks), axis=2) + 1e-06) / code_limit).astype(jnp.bfloat16)
    encoded = (blocks / scales.astype(jnp.float32)[:, :, None]).astype(jnp.bfloat16)
    return (encoded.reshape(row_count, -1), scales)


def expand(encoded, scales):
    row_count = encoded.shape[0]
    blocks = (
        encoded.astype(jnp.float32).reshape(row_count, -1, BLOCK)
        * scales.astype(jnp.float32)[:, :, None]
    )
    return blocks.reshape(row_count, -1)


def positions_of(segment_ids):
    token_count = segment_ids.shape[0]
    token_index = jnp.arange(token_count, dtype=jnp.int32)
    change = jnp.concatenate([jnp.ones((1,), dtype=bool), segment_ids[1:] != segment_ids[:-1]])
    offset = lax.cummax(jnp.where(change, token_index, jnp.zeros_like(token_index)), axis=0)
    return token_index - offset


def rotate(values, positions):
    half_dim = values.shape[-1] // 2
    inv_freq = rope_base ** (-(jnp.arange(half_dim, dtype=jnp.float32) * 2.0) / (2 * half_dim))
    angles = positions.astype(jnp.float32)[:, None] * inv_freq[None, :]
    cosine = jnp.cos(angles)[:, None, :]
    sine_vals = jnp.sin(angles)[:, None, :]
    first_half = values[..., :half_dim].astype(jnp.float32)
    second = values[..., half_dim:].astype(jnp.float32)
    return jnp.concatenate(
        [first_half * cosine - second * sine_vals, second * cosine + first_half * sine_vals],
        axis=-1,
    )


def attend(queries, chosen_keys, chosen_values, segment_ids):
    token_count = queries.shape[0]
    token_index = jnp.arange(token_count, dtype=jnp.int32)
    scores = jnp.einsum(
        "qhd,khd->hqk", queries, chosen_keys, preferred_element_type=jnp.float32
    ) / math.sqrt(queries.shape[2])
    allowed = (token_index[None, :] <= token_index[:, None]) & (
        segment_ids[:, None] == segment_ids[None, :]
    )
    scores = jnp.where(allowed[None], scores, -1e30)
    row_max = jnp.max(scores, axis=2, keepdims=True)
    weights = jnp.exp(scores - row_max)
    probabilities = (weights / jnp.sum(weights, axis=2, keepdims=True)).astype(jnp.bfloat16)
    outputs = jnp.einsum(
        "hqk,khd->qhd", probabilities, chosen_values, preferred_element_type=jnp.float32
    )
    return outputs.astype(jnp.bfloat16).reshape(token_count, -1)


def per_device_general(residual, norm_gain, segment_ids, w_query, w_key, w_value, w_out):
    own_rows = residual.shape[0]
    mean_square = jnp.mean(residual * residual, axis=1, keepdims=True)
    normed = residual * lax.rsqrt(mean_square + 1e-05) * norm_gain[None, :]
    encoded, scales = quantize(normed)
    token_count = segment_ids.shape[0]
    head_cols = w_query.shape[1]
    inputs = expand(
        lax.all_gather(encoded, "tp", axis=0, tiled=True),
        lax.all_gather(scales, "tp", axis=0, tiled=True),
    ).astype(jnp.bfloat16)
    query_part = jnp.dot(inputs, w_query, preferred_element_type=jnp.float32).astype(jnp.bfloat16)
    key_part = jnp.dot(inputs, w_key, preferred_element_type=jnp.float32).astype(jnp.bfloat16)
    value_part = jnp.dot(inputs, w_value, preferred_element_type=jnp.float32).astype(jnp.bfloat16)
    key_lin, value_lin = (
        lax.all_gather(key_part, "tp", axis=1, tiled=True),
        lax.all_gather(value_part, "tp", axis=1, tiled=True),
    )
    positions = positions_of(segment_ids)
    local_heads = head_cols // HD
    queries = rotate(query_part.reshape(token_count, local_heads, HD), positions).astype(
        jnp.bfloat16
    )
    key_heads = key_lin.reshape(token_count, HD, KVH).transpose(0, 2, 1)
    rotated_keys = rotate(key_heads, positions).astype(jnp.bfloat16)
    values = value_lin.reshape(token_count, HD, KVH).transpose(0, 2, 1)
    head_ids = (lax.axis_index("tp") * local_heads + jnp.arange(local_heads, dtype=jnp.int32)) // (
        QH // KVH
    )
    chosen_keys = jnp.take(rotated_keys, head_ids, axis=1)
    chosen_values = jnp.take(values, head_ids, axis=1)
    attended = attend(queries, chosen_keys, chosen_values, segment_ids)
    partial_value = jnp.dot(attended, w_out, preferred_element_type=jnp.float32)
    part_codes, part_scales = quantize(partial_value)
    got_codes, got_scales = (
        lax.all_to_all(part_codes, "tp", split_axis=0, concat_axis=0, tiled=True),
        lax.all_to_all(part_scales, "tp", split_axis=0, concat_axis=0, tiled=True),
    )
    sources = lax.axis_size("tp")
    owner_terms = expand(got_codes, got_scales).reshape(sources, own_rows, -1)
    summed = jnp.sum(owner_terms, axis=0)
    return residual + summed


def solution(mesh):
    in_specs = (
        P(("groups", "tp"), None),
        P(),
        P("groups"),
        P(None, "tp"),
        P(None, "tp"),
        P(None, "tp"),
        P("tp", None),
    )
    out_specs = P(("groups", "tp"), None)
    body = per_device_kernel if mesh.shape["tp"] == N else per_device_general
    return jax.shard_map(
        body, mesh=mesh, in_specs=in_specs, out_specs=out_specs, check_vma=False
    )
```

```python
import functools
import math

import jax
import jax.numpy as jnp
from jax import lax
from jax.experimental import pallas as pl
from jax.experimental.pallas import tpu as pltpu
from jax.sharding import PartitionSpec as P

QH = 64
KVH = 8
HD = 128
BLOCK = 128


code_limit = 448.0
rope_base = 500000.0

NZ, NY, NC = 4, 2, 2
N = NZ * NY * NC
OWN = 4
SUB = 16 // OWN
KC = 4
RC = 8
CORE_LAG, Y_LAG, Z_LAG = 2, 4, 7


def one_hot(condition):
    return jnp.where(condition, 1.0, 0.0).astype(jnp.bfloat16)


def token_of_row(row):
    core, y, z, tok = row // 32, (row // 16) % 2, (row // 4) % 4, row % 4
    return ((z * NY + y) * NC + core) * OWN + tok


def dot(a, b):
    return jnp.dot(a, b, preferred_element_type=jnp.float32)


def dot_t(a, b):
    return lax.dot_general(a, b, (((1,), (1,)), ((), ())), preferred_element_type=jnp.float32)


def layer_kernel(
    residual, gain, segments, w_query, w_key, w_value, w_out, out,
    pack, gathered, wq, wkv, wo, q_acc, kv_acc, kv_out, kv_in, attended,
    core_own, core_out, core_in, y_own, y_out, y_in, z_out, z_in, total,
    w_sem, wo_sem, g_recv, g_zsend, g_ysend, g_csend, kv_send, kv_recv,
    c_send, c_recv, y_send, y_recv, z_send, z_recv,
):
    depth = w_query.shape[0]
    chunk = depth // KC
    width = chunk // SUB
    cols = w_out.shape[1] // RC
    quarter = cols // SUB
    tokens = N * OWN
    heads = w_query.shape[1] // HD
    kv_cols = w_key.shape[0]

    me = lax.axis_index("tp")
    z, y, core = me // 4, (me // 2) % 2, me % 2
    y_peer = (z * NY + (1 - y)) * NC + core
    core_peer = (z * NY + y) * NC + (1 - core)

    def at_z(zz):
        return (zz * NY + y) * NC + core

    def weight_copies(k):
        rows = pl.ds(pl.multiple_of(k * chunk, chunk), chunk)
        return [
            pltpu.make_async_copy(w_query.at[rows], wq.at[rows], w_sem.at[0, k]),
            pltpu.make_async_copy(w_key.at[:, rows], wkv.at[k, :kv_cols], w_sem.at[1, k]),
            pltpu.make_async_copy(w_value.at[:, rows], wkv.at[k, kv_cols:], w_sem.at[2, k]),
        ]

    def out_copy(j):
        return pltpu.make_async_copy(
            w_out.at[:, pl.ds(pl.multiple_of(j * cols, cols), cols)], wo.at[j], wo_sem.at[j]
        )

    def remote(src, dst, send, recv, peer):
        return pltpu.make_async_remote_copy(
            src_ref=src, dst_ref=dst, send_sem=send, recv_sem=recv,
            device_id={"tp": peer}, device_id_type=pl.DeviceIdType.MESH,
        )

    def piece_copy(k, src, send, peer):
        return remote(gathered.at[k, src], gathered.at[k, src], send, g_recv.at[k, src], peer)

    def z_copy(k, d):
        return piece_copy(k, me, g_zsend.at[k, d - 1], at_z(lax.rem(z + d, NZ)))

    def near_line(d):
        return jnp.logical_not(
            ((z == 0) & (d == NZ - 1)) | ((z == NZ - 1) & (d == 1))
        )

    inner = (z == 1) | (z == 2)
    far = jnp.where(z == 1, NZ - 1, 0)
    beyond = jnp.where(z == 1, 0, NZ - 1)

    def relay_copy(k):
        return piece_copy(k, at_z(far), g_zsend.at[k, NZ - 1], at_z(beyond))

    def y_copy(k, d):
        return piece_copy(k, at_z(lax.rem(z + d, NZ)), g_ysend.at[k, d], y_peer)

    def c_copy(k, d, yy):
        src = (lax.rem(z + d, NZ) * NY + yy) * NC + core
        return piece_copy(k, src, g_csend.at[k, d, yy], core_peer)

    barrier = pltpu.get_barrier_semaphore()

    line = [at_z(lax.rem(z + d, NZ)) for d in range(1, NZ)]
    for peer in [y_peer, core_peer] + line:
        pl.semaphore_signal(
            barrier, inc=1, device_id={"tp": peer}, device_id_type=pl.DeviceIdType.MESH
        )
    for k in range(KC):
        for copy in weight_copies(k):
            copy.start()

    values = residual[...]
    inv = lax.rsqrt(jnp.mean(values * values, axis=1, keepdims=True) + 1e-05)
    for k in range(KC):
        for q in range(SUB):
            at = k * chunk + q * width
            pack[k, q * OWN:(q + 1) * OWN, :] = (
                residual[:, at:at + width] * inv * gain[:, at:at + width]
            )
        gathered[k, me] = pack[k].astype(jnp.bfloat16)
    pl.semaphore_wait(barrier, NZ + 1)

    def send_own(k, carry):
        c_copy(k, 0, y).start()
        y_copy(k, 0).start()
        for d in (1, 2, 3):
            pl.when(near_line(d))(lambda: z_copy(k, d).start())
        return carry

    lax.fori_loop(0, KC, send_own, 0)

    q_acc[...] = jnp.zeros_like(q_acc)
    kv_acc[...] = jnp.zeros_like(kv_acc)

    row_i = lax.broadcasted_iota(jnp.int32, (tokens, tokens), 0)
    col_i = lax.broadcasted_iota(jnp.int32, (tokens, tokens), 1)
    row_tok, col_tok = token_of_row(row_i), token_of_row(col_i)
    seg_plain = jnp.broadcast_to(segments[...], (tokens, tokens))
    seg_col = jnp.sum(jnp.where(col_i == row_tok, seg_plain, 0), axis=1, keepdims=True)
    seg_col_plain = jnp.sum(jnp.where(col_i == row_i, seg_plain, 0), axis=1, keepdims=True)
    seg_row = jnp.sum(jnp.where(row_i == col_tok, seg_col_plain, 0), axis=0, keepdims=True)
    start_col = jnp.sum(jnp.where(seg_plain < seg_col, 1, 0), axis=1, keepdims=True)
    start_row = jnp.sum(jnp.where(seg_col_plain < seg_row, 1, 0), axis=0, keepdims=True)
    allowed = (col_tok <= row_tok) & (seg_col == seg_row)
    half = HD // 2
    pos_col = (row_tok[:, :half] - start_col).astype(jnp.float32)
    pos_row = (col_tok[:half, :] - start_row).astype(jnp.float32)
    log_base = math.log(rope_base)
    freq_lane = jnp.exp(col_i[:, :half].astype(jnp.float32) * (-2.0 * log_base / HD))
    freq_row = jnp.exp(row_i[:half, :].astype(jnp.float32) * (-2.0 * log_base / HD))
    cos_q, sin_q = jnp.cos(pos_col * freq_lane), jnp.sin(pos_col * freq_lane)
    cos_k, sin_k = jnp.cos(pos_row * freq_row), jnp.sin(pos_row * freq_row)

    pr = lax.broadcasted_iota(jnp.int32, (N * 16, N * 16), 0)
    pc = lax.broadcasted_iota(jnp.int32, (N * 16, N * 16), 1)
    tok = token_of_row(pr % tokens)
    order = one_hot(pc == (tok // OWN) * 16 + (pr // tokens) * OWN + tok % OWN)

    def gather_step(s, carry):
        @pl.when(s < KC)
        def _():
            order_z = (
                jnp.where(z == 0, 1, z - 1),
                jnp.where(z == 3, 1, jnp.where(z == 2, 3, 2)),
                jnp.where(z < 2, 3, 0),
            )
            for i, zz in enumerate(order_z):
                d = lax.rem(zz - z + NZ, NZ)
                piece_copy(s, at_z(zz), g_zsend.at[s, 0], y_peer).wait_recv()
                if i == 2:
                    pl.when(inner)(lambda: relay_copy(s).start())
                y_copy(s, d).start()
                c_copy(s, d, y).start()

        @pl.when((s >= 1) & (s < KC + 1))
        def _():
            k = s - 1
            for d in range(NZ):
                src = (lax.rem(z + d, NZ) * NY + (1 - y)) * NC + core
                piece_copy(k, src, g_zsend.at[k, 0], y_peer).wait_recv()
                c_copy(k, d, 1 - y).start()
            for i in range(RC // KC):
                out_copy(k * (RC // KC) + i).start()

        @pl.when(s >= 2)
        def _():
            k = s - 2
            rows = sorted_rows(k)
            add_keys(k, rows)
            add_queries(k, rows)

        return carry

    def sorted_rows(k):
        for d in range(N // 2):
            src = d * NC + (1 - core)
            piece_copy(k, src, g_zsend.at[k, 0], y_peer).wait_recv()
        for copy in weight_copies(k):
            copy.wait()
        return dot(order, gathered[k].reshape(N * 16, width)).astype(jnp.bfloat16)

    def add_keys(k, rows):
        for q in range(SUB):
            lhs = rows[q * tokens:(q + 1) * tokens]
            kv_acc[...] += dot_t(wkv[k, :, q * width:(q + 1) * width], lhs)

    def add_queries(k, rows):
        for q in range(SUB):
            lhs = rows[q * tokens:(q + 1) * tokens]
            at = pl.ds(pl.multiple_of(k * chunk + q * width, width), width)
            q_acc[...] += dot(lhs, wq[at, :])

    lax.fori_loop(0, KC + 1, gather_step, 0)
    last_rows = sorted_rows(KC - 1)
    add_keys(KC - 1, last_rows)

    sr = lax.broadcasted_iota(jnp.int32, (HD, HD), 0)
    sc = lax.broadcasted_iota(jnp.int32, (HD, HD), 1)
    source = ((sr // 8) % 2) * kv_cols + (sr % 8) * KVH + sr // 16
    turned = dot(one_hot(sc == source), kv_acc[...].astype(jnp.bfloat16))
    turned = jnp.concatenate([turned, turned], axis=1).astype(jnp.bfloat16)
    kv_out[...] = turned.reshape(KVH, 16, HD)

    def kv_copy(d):
        peer = lax.rem(me + d, N)
        return remote(kv_out.at[peer // 2], kv_in.at[me], kv_send.at[d], kv_recv.at[me], peer)

    def kv_start(d, carry):
        kv_copy(d).start()
        return carry

    lax.fori_loop(1, N, kv_start, 0)
    kv_in[me] = kv_out[me // 2]
    add_queries(KC - 1, last_rows)

    scale = 1.0 / math.sqrt(HD)
    queries = []
    for h in range(heads):
        lin = q_acc[:, h * HD:(h + 1) * HD].astype(jnp.bfloat16).astype(jnp.float32)
        a, b = lin[:, :half], lin[:, half:]
        queries.append(
            jnp.concatenate([a * cos_q - b * sin_q, b * cos_q + a * sin_q], axis=1)
        )

    def kv_wait(d, carry):
        src = lax.rem(me + d, N)
        remote(kv_out.at[0], kv_in.at[src], kv_send.at[d], kv_recv.at[src], src).wait_recv()
        return carry

    lax.fori_loop(1, N, kv_wait, 0)
    kv = kv_in[...].astype(jnp.float32)
    keys = kv[:, :8, :tokens].reshape(HD, tokens)
    vals = kv[:, 8:, :tokens].reshape(HD, tokens).astype(jnp.bfloat16)
    a, b = keys[:half], keys[half:]
    keys = jnp.concatenate([a * cos_k - b * sin_k, b * cos_k + a * sin_k], axis=0)
    keys = keys.astype(jnp.bfloat16)
    stacked = jnp.concatenate(queries, axis=0).astype(jnp.bfloat16)
    scores = dot(stacked, keys) * scale
    scores = jnp.where(jnp.concatenate([allowed] * heads, axis=0), scores, -1e30)
    weights = jnp.exp(scores - jnp.max(scores, axis=1, keepdims=True))
    probs = (weights / jnp.sum(weights, axis=1, keepdims=True)).astype(jnp.bfloat16)
    mixed = dot_t(probs, vals).astype(jnp.bfloat16)
    for h in range(heads):
        attended[:, h * HD:(h + 1) * HD] = mixed[h * tokens:(h + 1) * tokens]

    zr = lax.broadcasted_iota(jnp.int32, (64, 64), 0)
    zc = lax.broadcasted_iota(jnp.int32, (64, 64), 1)
    by_z = one_hot(zc == ((zr // OWN) % SUB) * 16 + (zr // 16) * OWN + zr % OWN)

    def core_copy(j):
        return remote(core_out.at[j], core_in.at[j], c_send.at[j], c_recv.at[j], core_peer)

    def row_copy(j):
        return remote(y_out.at[j], y_in.at[j], y_send.at[j], y_recv.at[j], y_peer)

    def line_copy(j, d):
        zz = lax.rem(z + d, NZ)
        return remote(
            z_out.at[j, zz], z_in.at[j, z], z_send.at[j, d - 1], z_recv.at[j, z], at_z(zz)
        )

    def sum_step(s, carry):
        @pl.when(s < RC)
        def _():
            out_copy(s).wait()
            part = dot(attended[...], wo[s]).reshape(2, 32, cols)
            low, high = part[0], part[1]
            core_out[s] = jnp.where(core == 0, high, low).astype(jnp.bfloat16)
            core_copy(s).start()
            core_own[s] = jnp.where(core == 0, low, high)

        @pl.when((s >= CORE_LAG) & (s < RC + CORE_LAG))
        def _():
            j = s - CORE_LAG
            core_copy(j).wait_recv()
            both = core_own[j] + core_in[j].astype(jnp.float32)
            low, high = both[:16], both[16:]
            y_out[j] = jnp.where(y == 0, high, low).astype(jnp.bfloat16)
            row_copy(j).start()
            y_own[j] = jnp.where(y == 0, low, high)

        @pl.when((s >= Y_LAG) & (s < RC + Y_LAG))
        def _():
            j = s - Y_LAG
            row_copy(j).wait_recv()
            both = y_own[j] + y_in[j].astype(jnp.float32)
            stacked = jnp.concatenate(
                [both[:, q * quarter:(q + 1) * quarter] for q in range(SUB)], axis=0
            )
            sorted_rows = dot(by_z, stacked.astype(jnp.bfloat16)).astype(jnp.bfloat16)
            z_out[j] = sorted_rows.reshape(NZ, 16, quarter)
            for d in (1, 2, 3):
                line_copy(j, d).start()

        @pl.when(s >= Z_LAG)
        def _():
            j = s - Z_LAG
            summed = z_out[j, z].astype(jnp.float32)
            for d in (1, 2, 3):
                zz = lax.rem(z + d, NZ)
                remote(
                    z_out.at[j, zz], z_in.at[j, zz], z_send.at[j, 0], z_recv.at[j, zz], at_z(zz)
                ).wait_recv()
                summed = summed + z_in[j, zz].astype(jnp.float32)
            total[j] = summed
            for q in range(SUB):
                at = pl.ds(pl.multiple_of(j * cols + q * quarter, quarter), quarter)
                out[:, at] = total[j, q * OWN:(q + 1) * OWN, :]

        return carry

    lax.fori_loop(0, RC + Z_LAG, sum_step, 0)

    def sent_gather(k, carry):
        pl.when(inner)(lambda: relay_copy(k).wait_send())
        for d in range(NZ):
            if d > 0:
                pl.when(near_line(d))(lambda: z_copy(k, d).wait_send())
            y_copy(k, d).wait_send()
            c_copy(k, d, 0).wait_send()
            c_copy(k, d, 1).wait_send()
        return carry

    def sent_kv(d, carry):
        kv_copy(d).wait_send()
        return carry

    def sent_sum(j, carry):
        core_copy(j).wait_send()
        row_copy(j).wait_send()
        for d in (1, 2, 3):
            line_copy(j, d).wait_send()
        return carry

    lax.fori_loop(0, KC, sent_gather, 0)
    lax.fori_loop(1, N, sent_kv, 0)
    lax.fori_loop(0, RC, sent_sum, 0)


def per_device_kernel(residual, norm_gain, segment_ids, w_query, w_key, w_value, w_out):
    depth, head_cols = w_query.shape
    kv_cols = w_key.shape[1]
    tokens = segment_ids.shape[0]
    width = depth // KC // SUB
    cols = depth // RC
    quarter = cols // SUB
    f32, bf16 = jnp.float32, jnp.bfloat16
    vmem = pl.BlockSpec(memory_space=pltpu.VMEM)
    hbm = pl.BlockSpec(memory_space=pl.ANY)
    dma = pltpu.SemaphoreType.DMA
    summed = pl.pallas_call(
        layer_kernel,
        out_shape=jax.ShapeDtypeStruct(residual.shape, f32),
        in_specs=[vmem, vmem, vmem, hbm, hbm, hbm, hbm],
        out_specs=vmem,
        scratch_shapes=[
            pltpu.VMEM((KC, 16, width), f32),
            pltpu.VMEM((KC, N, 16, width), bf16),
            pltpu.VMEM((depth, head_cols), bf16),
            pltpu.VMEM((KC, 2 * kv_cols, depth // KC), bf16),
            pltpu.VMEM((RC, head_cols, cols), bf16),
            pltpu.VMEM((tokens, head_cols), f32),
            pltpu.VMEM((2 * kv_cols, tokens), f32),
            pltpu.VMEM((KVH, 16, HD), bf16),
            pltpu.VMEM((N, 16, HD), bf16),
            pltpu.VMEM((tokens, head_cols), bf16),
            pltpu.VMEM((RC, 32, cols), f32),
            pltpu.VMEM((RC, 32, cols), bf16),
            pltpu.VMEM((RC, 32, cols), bf16),
            pltpu.VMEM((RC, 16, cols), f32),
            pltpu.VMEM((RC, 16, cols), bf16),
            pltpu.VMEM((RC, 16, cols), bf16),
            pltpu.VMEM((RC, NZ, 16, quarter), bf16),
            pltpu.VMEM((RC, NZ, 16, quarter), bf16),
            pltpu.VMEM((RC, 16, quarter), f32),
            dma((3, KC)),
            dma((RC,)),
            dma((KC, N)),
            dma((KC, NZ)),
            dma((KC, NZ)),
            dma((KC, NZ, NY)),
            dma((N,)),
            dma((N,)),
            dma((RC,)),
            dma((RC,)),
            dma((RC,)),
            dma((RC,)),
            dma((RC, NZ - 1)),
            dma((RC, NZ)),
        ],
        compiler_params=pltpu.CompilerParams(
            collective_id=0, has_side_effects=True, vmem_limit_bytes=60 * 1024 * 1024
        ),
        name="sublayer",
    )(
        residual, norm_gain.reshape(1, -1), segment_ids.reshape(1, -1),
        w_query, w_key.T, w_value.T, w_out,
    )
    return residual + summed


def quantize(values):
    row_count = values.shape[0]
    blocks = values.reshape(row_count, -1, BLOCK)
    scales = ((jnp.max(jnp.abs(blocks), axis=2) + 1e-06) / code_limit).astype(jnp.bfloat16)
    encoded = (blocks / scales.astype(jnp.float32)[:, :, None]).astype(jnp.bfloat16)
    return (encoded.reshape(row_count, -1), scales)


def expand(encoded, scales):
    row_count = encoded.shape[0]
    blocks = (
        encoded.astype(jnp.float32).reshape(row_count, -1, BLOCK)
        * scales.astype(jnp.float32)[:, :, None]
    )
    return blocks.reshape(row_count, -1)


def positions_of(segment_ids):
    token_count = segment_ids.shape[0]
    token_index = jnp.arange(token_count, dtype=jnp.int32)
    change = jnp.concatenate([jnp.ones((1,), dtype=bool), segment_ids[1:] != segment_ids[:-1]])
    offset = lax.cummax(jnp.where(change, token_index, jnp.zeros_like(token_index)), axis=0)
    return token_index - offset


def rotate(values, positions):
    half_dim = values.shape[-1] // 2
    inv_freq = rope_base ** (-(jnp.arange(half_dim, dtype=jnp.float32) * 2.0) / (2 * half_dim))
    angles = positions.astype(jnp.float32)[:, None] * inv_freq[None, :]
    cosine = jnp.cos(angles)[:, None, :]
    sine_vals = jnp.sin(angles)[:, None, :]
    first_half = values[..., :half_dim].astype(jnp.float32)
    second = values[..., half_dim:].astype(jnp.float32)
    return jnp.concatenate(
        [first_half * cosine - second * sine_vals, second * cosine + first_half * sine_vals],
        axis=-1,
    )


def attend(queries, chosen_keys, chosen_values, segment_ids):
    token_count = queries.shape[0]
    token_index = jnp.arange(token_count, dtype=jnp.int32)
    scores = jnp.einsum(
        "qhd,khd->hqk", queries, chosen_keys, preferred_element_type=jnp.float32
    ) / math.sqrt(queries.shape[2])
    allowed = (token_index[None, :] <= token_index[:, None]) & (
        segment_ids[:, None] == segment_ids[None, :]
    )
    scores = jnp.where(allowed[None], scores, -1e30)
    row_max = jnp.max(scores, axis=2, keepdims=True)
    weights = jnp.exp(scores - row_max)
    probabilities = (weights / jnp.sum(weights, axis=2, keepdims=True)).astype(jnp.bfloat16)
    outputs = jnp.einsum(
        "hqk,khd->qhd", probabilities, chosen_values, preferred_element_type=jnp.float32
    )
    return outputs.astype(jnp.bfloat16).reshape(token_count, -1)


def per_device_general(residual, norm_gain, segment_ids, w_query, w_key, w_value, w_out):
    own_rows = residual.shape[0]
    mean_square = jnp.mean(residual * residual, axis=1, keepdims=True)
    normed = residual * lax.rsqrt(mean_square + 1e-05) * norm_gain[None, :]
    encoded, scales = quantize(normed)
    token_count = segment_ids.shape[0]
    head_cols = w_query.shape[1]
    inputs = expand(
        lax.all_gather(encoded, "tp", axis=0, tiled=True),
        lax.all_gather(scales, "tp", axis=0, tiled=True),
    ).astype(jnp.bfloat16)
    query_part = jnp.dot(inputs, w_query, preferred_element_type=jnp.float32).astype(jnp.bfloat16)
    key_part = jnp.dot(inputs, w_key, preferred_element_type=jnp.float32).astype(jnp.bfloat16)
    value_part = jnp.dot(inputs, w_value, preferred_element_type=jnp.float32).astype(jnp.bfloat16)
    key_lin, value_lin = (
        lax.all_gather(key_part, "tp", axis=1, tiled=True),
        lax.all_gather(value_part, "tp", axis=1, tiled=True),
    )
    positions = positions_of(segment_ids)
    local_heads = head_cols // HD
    queries = rotate(query_part.reshape(token_count, local_heads, HD), positions).astype(
        jnp.bfloat16
    )
    key_heads = key_lin.reshape(token_count, HD, KVH).transpose(0, 2, 1)
    rotated_keys = rotate(key_heads, positions).astype(jnp.bfloat16)
    values = value_lin.reshape(token_count, HD, KVH).transpose(0, 2, 1)
    head_ids = (lax.axis_index("tp") * local_heads + jnp.arange(local_heads, dtype=jnp.int32)) // (
        QH // KVH
    )
    chosen_keys = jnp.take(rotated_keys, head_ids, axis=1)
    chosen_values = jnp.take(values, head_ids, axis=1)
    attended = attend(queries, chosen_keys, chosen_values, segment_ids)
    partial_value = jnp.dot(attended, w_out, preferred_element_type=jnp.float32)
    part_codes, part_scales = quantize(partial_value)
    got_codes, got_scales = (
        lax.all_to_all(part_codes, "tp", split_axis=0, concat_axis=0, tiled=True),
        lax.all_to_all(part_scales, "tp", split_axis=0, concat_axis=0, tiled=True),
    )
    sources = lax.axis_size("tp")
    owner_terms = expand(got_codes, got_scales).reshape(sources, own_rows, -1)
    summed = jnp.sum(owner_terms, axis=0)
    return residual + summed


def solution(mesh):
    in_specs = (
        P(("groups", "tp"), None),
        P(),
        P("groups"),
        P(None, "tp"),
        P(None, "tp"),
        P(None, "tp"),
        P("tp", None),
    )
    out_specs = P(("groups", "tp"), None)
    body = per_device_kernel if mesh.shape["tp"] == N else per_device_general
    return jax.shard_map(
        body, mesh=mesh, in_specs=in_specs, out_specs=out_specs, check_vma=False
    )
```
